256 devices in a mesh: seq: 64 (over z, y, x_hi), head: 4 (over x_lo, core).
Axes of the slice: x: 4 (x_hi: 2, x_lo: 2; x = x_hi * 2 + x_lo), y: 4, z: 8, core: 2. Of those that a mesh axis runs over, the one named last changes fastest.
Arguments:
- queries: bfloat16 [32768, 12, 128], P('seq', 'head'), may hold values from -130 to 130
- keys: bfloat16 [32768, 12, 128], P('seq', 'head'), may hold values from -10 to 10
- values: bfloat16 [32768, 12, 128], P('seq', 'head'), may hold values from -8 to 8
- w_out: bfloat16 [768, 768], P('head'), may hold values from -0.21875 to 0.21875
Outputs:
- mixed: bfloat16 [32768, 12, 128], P('seq', 'head')
The draws below stay inside these ranges and needn't reach their ends.
All inputs are finite; a program needn't handle non-finite values.
Results may differ from the reference program's by a relative error of at most 0.03.
Values may be sent and summed in bfloat16 or wider, within the bound.
No kernel may reach another device: no remote copies, remote signals or barrier semaphores. Data moves between devices by JAX's collectives and lax.ppermute only.
A program may use at most 64 MiB of HBM per device.

```python
import math
import jax
import jax.numpy as jnp
from jax import lax

HEADS = 12
HEAD_DIM = 64
D = 768
NR = 128
LEVELS = 3
TOKENS = 65536
POOL = 1024
N_HEAD = 4


def paired_layout(source):
    return source.reshape(TOKENS // 2, 2, HEADS, HEAD_DIM).transpose(0, 2, 1, 3).reshape(TOKENS // 2, HEADS, 2 * HEAD_DIM)


def draw_queries(key, part):
    key = jax.random.fold_in(key, 11)
    first_key = jax.random.fold_in(key, 0)
    result = jnp.clip(jax.random.normal(first_key, (TOKENS, D), jnp.float32), -5.0, 5.0)
    return paired_layout(result).astype(jnp.bfloat16)


def draw_keys(key, part):
    key = jax.random.fold_in(key, 23)
    first_key, second_key = jax.random.split(key)
    scale = jnp.exp(jax.random.uniform(second_key, (TOKENS, 1), jnp.float32, jnp.log(0.25), jnp.log(2.5)))
    result = jnp.clip(jax.random.normal(first_key, (TOKENS, D), jnp.float32), -4.0, 4.0) * scale
    return paired_layout(result).astype(jnp.bfloat16)


def block_scale(stream_key, shape, shards, least, high):
    def one(axis_at, parts):
        heights = jax.random.uniform(jax.random.fold_in(jax.random.fold_in(stream_key, 6), axis_at), (parts,), jnp.float32, least / len(shards), high / len(shards))
        return jnp.repeat(jnp.exp(heights), shape[axis_at] // parts).reshape((-1,) + (1,) * (len(shape) - axis_at - 1))

    factor_of = one(*shards[0])
    for cut in shards[1:]:
        factor_of = factor_of * one(*cut)
    return factor_of


def noise(own_key, shape, scale, bound, cuts=(), kind=jnp.bfloat16):
    values = jax.random.normal(own_key, shape, jnp.float32) * scale
    if len(cuts) > 0:
        values = block_scale(own_key, shape, cuts, -0.22, 0.18) * values
    return jnp.clip(values, min=-bound, max=bound).astype(kind)


def setup_inputs(seed: int = 0) -> dict:
    streams_of = jax.random.split(jax.random.key(seed), 5)
    queries = draw_queries(jax.random.fold_in(streams_of[4], 71), 0)
    keys = draw_keys(jax.random.fold_in(streams_of[4], 71), 0)
    values = noise(streams_of[2], (TOKENS // 2, HEADS, 2 * HEAD_DIM), 2.0, 8.0, ((0, 64), (1, 4)))
    w_out = noise(streams_of[3], (D, D), D ** -0.5, 0.21875, ((0, 4),))
    return dict(queries=queries, keys=keys, values=values, w_out=w_out)


def pool_rows(source, factor, averaged):
    summed = source.astype(jnp.float32).reshape(source.shape[0] // factor, factor, source.shape[1]).sum(axis=1)
    if averaged:
        summed = summed * (1.0 / factor)
    else:
        summed = summed * (factor ** -0.5)
    return summed.astype(jnp.bfloat16)


def band_mask(level_index):
    query_row = jnp.arange(NR, dtype=jnp.int32)[:, None]
    key_pos = jnp.arange(3 * NR, dtype=jnp.int32)[None, :] - NR
    if level_index == 0:
        return jnp.ones((NR, 3 * NR), dtype=jnp.bool_)
    block_halfway = NR // 2
    parent = query_row // block_halfway
    return (key_pos < block_halfway * (parent - 1)) | (key_pos >= block_halfway * (parent + 2))


def softmax_terms(grouped_queries, banded_key_rows, banded_value_rows, keep_mask):
    logit_scores = jnp.einsum('jwn,jon->jwo', grouped_queries.astype(jnp.float32), banded_key_rows.astype(jnp.float32))
    logit_scores = logit_scores * (HEAD_DIM ** -0.5)
    logit_scores = jnp.where(keep_mask, logit_scores, -jnp.inf)
    maxima = jnp.max(logit_scores, axis=-1)
    probs = jnp.where(keep_mask, jnp.exp(logit_scores - maxima[..., None]), 0.0)
    totals = jnp.sum(probs, axis=-1)
    attention_weights = probs.astype(jnp.bfloat16)
    weighted_values = jnp.einsum('rsn,rng->rsg', attention_weights.astype(jnp.float32), banded_value_rows.astype(jnp.float32))
    return weighted_values, totals, maxima


def band_level(query_rows, key_rows, value_rows, keep_mask):
    row_count = query_rows.shape[0]
    blocks = row_count // NR
    per_step = math.gcd(blocks, 32)
    groups = blocks // per_step
    key_ext = jnp.concatenate([key_rows[-NR:], key_rows, key_rows[:NR]], axis=0)
    value_ext = jnp.concatenate([value_rows[-NR:], value_rows, value_rows[:NR]], axis=0)
    query_blocks = query_rows.reshape(groups, per_step, NR, query_rows.shape[1])

    def attend_group(element):
        grouped_queries, group_index = element
        offset = group_index * (per_step * NR)
        key_window = lax.dynamic_slice_in_dim(key_ext, offset, (per_step + 2) * NR, 0).reshape(per_step + 2, NR, -1)
        value_window = lax.dynamic_slice_in_dim(value_ext, offset, (per_step + 2) * NR, 0).reshape(per_step + 2, NR, -1)
        banded_key_rows = jnp.concatenate([key_window[:per_step], key_window[1:per_step + 1], key_window[2:]], axis=1)
        banded_value_rows = jnp.concatenate([value_window[:per_step], value_window[1:per_step + 1], value_window[2:]], axis=1)
        return softmax_terms(grouped_queries, banded_key_rows, banded_value_rows, keep_mask)

    weighted_values, totals, maxima = lax.map(attend_group, (query_blocks, jnp.arange(groups, dtype=jnp.int32)))
    return weighted_values.reshape(row_count, -1), totals.reshape(row_count), maxima.reshape(row_count)


def coarse_level(query_rows, key_rows, value_rows):
    count = key_rows.shape[0]
    positions = jnp.arange(count, dtype=jnp.int32)
    distance = (positions[None, :] - positions[:, None]) % count
    keep_mask = (distance >= 2) & (distance <= count - 2)
    weighted_values, totals, maxima = softmax_terms(query_rows[None], key_rows[None], value_rows[None], keep_mask)
    return weighted_values[0], totals[0], maxima[0]


def combine_level(state, terms, factor):
    weighted_values, totals, maxima = state
    extra_weighted = jnp.repeat(terms[0], factor, axis=0)
    extra_totals = jnp.repeat(terms[1], factor, axis=0)
    extra_maxima = jnp.repeat(terms[2], factor, axis=0)
    largest = jnp.maximum(maxima, extra_maxima)
    keep_old = jnp.exp(maxima - largest)
    keep_new = jnp.exp(extra_maxima - largest)
    return (weighted_values * keep_old[:, None] + extra_weighted * keep_new[:, None],
            totals * keep_old + extra_totals * keep_new, largest)


def attend_head(query_head, key_head, value_head):
    state = band_level(query_head, key_head, value_head, band_mask(0))
    for level_index in range(1, LEVELS + 1):
        factor = 2 ** level_index
        terms = band_level(pool_rows(query_head, factor, False), pool_rows(key_head, factor, False),
                           pool_rows(value_head, factor, True), band_mask(level_index))
        state = combine_level(state, terms, factor)
    terms = coarse_level(pool_rows(query_head, POOL, False), pool_rows(key_head, POOL, False),
                         pool_rows(value_head, POOL, True))
    state = combine_level(state, terms, POOL)
    return (state[0] / state[1][:, None]).astype(jnp.bfloat16)


def head_major(source):
    return source.reshape(TOKENS // 2, HEADS, 2, HEAD_DIM).transpose(1, 0, 2, 3).reshape(HEADS, TOKENS, HEAD_DIM)


def reference(queries, keys, values, w_out):
    def per_head(element):
        return attend_head(element[0], element[1], element[2])

    attended = lax.map(per_head, (head_major(queries), head_major(keys), head_major(values)))
    attended = attended.transpose(1, 0, 2).reshape(TOKENS, D)
    group_width = D // N_HEAD
    total = jnp.zeros((TOKENS, D), jnp.float32)
    for group_index in range(N_HEAD):
        lower = group_index * group_width
        partial_sum = jnp.dot(attended[:, lower:lower + group_width], w_out[lower:lower + group_width],
                              preferred_element_type=jnp.float32).astype(jnp.bfloat16)
        total = total + lax.optimization_barrier(partial_sum).astype(jnp.float32)
    result = total.astype(jnp.bfloat16).reshape(TOKENS // 2, 2, HEADS, HEAD_DIM).transpose(0, 2, 1, 3)
    return result.reshape(TOKENS // 2, HEADS, 2 * HEAD_DIM)
```

```python
import functools
import math

import jax
import jax.numpy as jnp
from jax import lax
from jax.experimental import pallas as pl
from jax.experimental.pallas import tpu as pltpu
from jax.sharding import PartitionSpec as P

HEAD_DIM = 64
NR = 128
HALF = NR // 2
LANES = 2 * HEAD_DIM
LEVELS = 3
POOL = 1024
BF16 = jnp.bfloat16
F32 = jnp.float32
SCALE2 = HEAD_DIM ** (-0.5) * math.log2(math.e)
FAR = (HALF, NR - HALF // 2, NR - HALF // 4)
HALO_ROWS = 2 * HALF + sum(FAR)


def low_lanes(rows):
    return lax.broadcasted_iota(jnp.int32, (rows, LANES), 1) < HEAD_DIM


def swap(x):
    return pltpu.roll(x, HEAD_DIM, 1)


def swap16(x):
    return swap(x.astype(F32)).astype(BF16)


def fold_pairs(lo, hi):
    lo, hi = lo.astype(F32), hi.astype(F32)
    return jnp.where(low_lanes(lo.shape[0]), lo + swap(lo), hi + swap(hi))


def halve(scratch, x):
    rows = x.shape[0]
    scratch[pl.ds(0, rows), :] = x
    return scratch[pl.ds(0, rows // 2, 2), :] + scratch[pl.ds(1, rows // 2, 2), :]


def pooled_vk(sums, factor):
    scale = jnp.where(low_lanes(1), 1.0 / factor, factor ** (-0.5))
    return (sums * scale).astype(BF16)


def pooled_q(sums, factor):
    return jnp.where(low_lanes(sums.shape[0]), 0.0, sums * factor ** (-0.5)).astype(BF16)


def attend(lhs, keys, values):
    scores = lax.dot_general(lhs, keys, (((1,), (1,)), ((), ())), preferred_element_type=F32)
    largest = jnp.max(scores, axis=1, keepdims=True)
    probs = jnp.exp2((scores - largest) * SCALE2).astype(BF16)
    return (
        jnp.dot(probs, values, preferred_element_type=F32),
        jnp.broadcast_to(largest * SCALE2, (lhs.shape[0], LANES)),
    )


def merge(xa, ma, xb, mb):
    gap = ma - mb
    small = jnp.exp2(-jnp.abs(gap))
    first = gap >= 0
    return (
        xa * jnp.where(first, 1.0, small) + xb * jnp.where(first, small, 1.0),
        jnp.maximum(ma, mb),
    )


def ones_high(vk):
    return jnp.where(low_lanes(vk.shape[0]), vk, jnp.ones_like(vk))


def put_pairs(keys, values, block, k, v):
    at = block * NR
    keys[at : at + HALF, :] = k
    keys[at + HALF : at + NR, :] = swap16(k)
    values[at : at + HALF, :] = ones_high(v)
    values[at + HALF : at + NR, :] = ones_high(swap16(v))


def token_queries(q):
    lo = low_lanes(q.shape[0])
    zero = jnp.zeros_like(q)
    return jnp.concatenate([jnp.where(lo, q, zero), jnp.where(lo, swap16(q), zero)], axis=0)


def pooled_half(q_rows, window, at, c):
    if c == 0:
        pieces = [(at, HALF), (at + 2 * NR, NR)]
    else:
        pieces = [(at, NR), (at + 2 * NR + HALF, HALF)]
    vk = jnp.concatenate([window[start : start + size, :] for start, size in pieces], axis=0)
    return attend(q_rows, vk, ones_high(vk))


def prepare_kernel(k_ref, v_ref, vk1, vk2, vk3, top, low_out, high_out, scratch):
    k, v = k_ref[0], v_ref[0]
    rows = k.shape[0]
    sums = fold_pairs(v, k)
    vk1[0] = pooled_vk(sums, 2)
    sums = halve(scratch, sums)
    vk2[0] = pooled_vk(sums, 4)
    sums = halve(scratch, sums)
    vk3[0] = pooled_vk(sums, 8)
    top[0] = jnp.broadcast_to(pooled_vk(jnp.sum(sums, axis=0, keepdims=True), POOL), top.shape[1:])
    for out, low in ((low_out, True), (high_out, False)):
        at = 0
        pieces = [(k_ref, HALF), (v_ref, HALF), (vk1, FAR[0]), (vk2, FAR[1]), (vk3, FAR[2])]
        for index, (source, size) in enumerate(pieces):
            count = source.shape[1]
            if index < 2:
                start = 0 if low else count - size
            else:
                near = HALF >> (index - 2)
                start = near if low else count - near - size
            out[0, at : at + size, :] = source[0, start : start + size, :]
            at += size


def inner_kernel(q_ref, k_ref, v_ref, vk1, x0, m0, x1, m1, keys, values, scratch):
    blocks = q_ref.shape[1] // HALF
    for block in range(blocks):
        at = block * HALF
        put_pairs(keys, values, block, k_ref[0, at : at + HALF, :], v_ref[0, at : at + HALF, :])
    for block in range(1, blocks - 1):
        lhs = token_queries(q_ref[0, block * HALF : (block + 1) * HALF, :])
        window = slice((block - 1) * NR, (block + 2) * NR)
        x, m = attend(lhs, keys[window, :], values[window, :])
        out = slice((block - 1) * NR, block * NR)
        x0[0, out, :] = x
        m0[0, out, :] = m
    q = q_ref[0].astype(F32)
    q1 = pooled_q(q + swap(q), 2)
    rows = q1.shape[0]
    for block in range(1, rows // NR - 1):
        for c in range(2):
            at = block * NR + c * HALF
            x, m = pooled_half(q1[at : at + HALF], vk1.at[0], (block - 1) * NR, c)
            out = slice(at - NR, at - NR + HALF)
            x1[0, out, :] = x
            m1[0, out, :] = m


def outer_kernel(
    q_ref, k_ref, v_ref, vk1, vk2, vk3, low_in, high_in, top, x0_in, m0_in, x1_in, m1_in, place,
    att, keys, values, w1, w2, w3, qs, scratch, x0, m0, xs, ms, xt, mt,
):
    rows = q_ref.shape[1]
    blocks = rows // HALF
    pooled = ((w1, vk1), (w2, vk2), (w3, vk3))
    for window, own in pooled:
        count = own.shape[1]
        window[NR : NR + count, :] = own[0]
    for halo, low in ((low_in, True), (high_in, False)):
        k, v = halo[0, 0:HALF, :], halo[0, HALF : 2 * HALF, :]
        if low:
            put_pairs(keys, values, 0, k, v)
            put_pairs(keys, values, 1, k_ref[0, 0:HALF, :], v_ref[0, 0:HALF, :])
            put_pairs(keys, values, 2, k_ref[0, HALF : 2 * HALF, :], v_ref[0, HALF : 2 * HALF, :])
        else:
            put_pairs(keys, values, 3, k_ref[0, rows - 2 * HALF : rows - HALF, :], v_ref[0, rows - 2 * HALF : rows - HALF, :])
            put_pairs(keys, values, 4, k_ref[0, rows - HALF : rows, :], v_ref[0, rows - HALF : rows, :])
            put_pairs(keys, values, 5, k, v)
        sums = fold_pairs(v, k)
        at = 2 * HALF
        for level, (window, own) in enumerate(pooled, 1):
            near, far, count = HALF >> (level - 1), FAR[level - 1], own.shape[1]
            if level > 1:
                sums = halve(scratch, sums)
            close = pooled_vk(sums, 2**level)
            distant = halo[0, at : at + far, :]
            if low:
                window[0:far, :] = distant
                window[far:NR, :] = close
            else:
                window[NR + count : NR + count + near, :] = close
                window[NR + count + near : NR + count + NR, :] = distant
            at += far
    for block, window in ((0, 0), (blocks - 1, 3 * NR)):
        lhs = token_queries(q_ref[0, block * HALF : (block + 1) * HALF, :])
        x, m = attend(lhs, keys[window : window + 3 * NR, :], values[window : window + 3 * NR, :])
        x0[block * NR : (block + 1) * NR, :] = x
        m0[block * NR : (block + 1) * NR, :] = m
    q = q_ref[0].astype(F32)
    sums = q + swap(q)
    starts = (0, rows, rows + rows // 2)
    for level, (window, own) in enumerate(pooled, 1):
        count = own.shape[1]
        if level > 1:
            sums = halve(scratch, sums)
        qs[starts[level - 1] : starts[level - 1] + count, :] = pooled_q(sums, 2**level)
    q_top = pooled_q(jnp.broadcast_to(jnp.sum(sums, axis=0, keepdims=True), (16, LANES)), POOL)
    for level, (window, own) in enumerate(pooled, 1):
        count = own.shape[1]
        base = starts[level - 1]
        for block in range(count // NR):
            for c in range(2):
                at = base + block * NR + c * HALF
                if level == 1 and 0 < block < count // NR - 1:
                    inner = slice(at - NR, at - NR + HALF)
                    x, m = x1_in[0, inner, :], m1_in[0, inner, :]
                else:
                    x, m = pooled_half(qs[at : at + HALF, :], window, block * NR, c)
                xs[at : at + HALF, :] = x
                ms[at : at + HALF, :] = m
    vk = top[0]
    positions = vk.shape[0]
    own_place = place[0]
    scores = lax.dot_general(q_top, vk, (((1,), (1,)), ((), ())), preferred_element_type=F32)
    distance = lax.broadcasted_iota(jnp.int32, scores.shape, 1) - own_place
    distance = jnp.where(distance < 0, distance + positions, distance)
    keep = (distance >= 2) & (distance <= positions - 2)
    scores = jnp.where(keep, scores, -jnp.inf)
    largest = jnp.max(scores, axis=1, keepdims=True)
    probs = jnp.exp2((scores - largest) * SCALE2).astype(BF16)
    x = jnp.dot(probs, ones_high(vk), preferred_element_type=F32)[0:1, :]
    m = jnp.broadcast_to(largest * SCALE2, (16, LANES))[0:1, :]
    for level in (3, 2, 1):
        count = rows >> (level - 1)
        base = starts[level - 1]
        if level == 3:
            above, above_m = x, m
        else:
            above, above_m = xt[0:count, :], mt[0:count, :]
        merged, merged_m = merge(xs[base : base + count, :], ms[base : base + count, :], above, above_m)
        if level == 1:
            xs[0:count, :] = merged
            ms[0:count, :] = merged_m
        else:
            for half in range(2):
                xt[pl.ds(half, count, 2), :] = merged
                mt[pl.ds(half, count, 2), :] = merged_m
    lo = low_lanes(HALF)
    for block in range(blocks):
        above = xs[block * HALF : (block + 1) * HALF, :]
        above_m = ms[block * HALF : (block + 1) * HALF, :]
        halves = []
        for parity in range(2):
            if 0 < block < blocks - 1:
                at = (block - 1) * NR + parity * HALF
                own, own_m = x0_in[0, at : at + HALF, :], m0_in[0, at : at + HALF, :]
            else:
                at = block * NR + parity * HALF
                own, own_m = x0[at : at + HALF, :], m0[at : at + HALF, :]
            both, _ = merge(own, own_m, above, above_m)
            halves.append(both / swap(both))
        att[0, block * HALF : (block + 1) * HALF, :] = jnp.where(lo, halves[0], swap(halves[1])).astype(BF16)


def project_kernel(*refs):
    *sources, w_ref, out_ref = refs
    heads = out_ref.shape[0]
    att = [jnp.concatenate([source[i] for i in range(heads)], axis=1) for source in sources]
    for group in range(heads):
        column = slice(group * LANES, (group + 1) * LANES)
        total = None
        for index, rows in enumerate(att):
            term = jnp.dot(rows, w_ref[index, :, column], preferred_element_type=F32)
            total = term if total is None else total + term
        out_ref[group] = total.astype(BF16)


def head_block(*shape):
    return pl.BlockSpec((1,) + shape, lambda h: (h,) + (0,) * len(shape))


def ring(count, step):
    return [(i, (i + step) % count) for i in range(count)]


def arrange_kernel(*refs):
    *sources, out_ref = refs
    for index, source in enumerate(sources):
        heads = source.shape[0] // HEAD_DIM
        for head in range(heads):
            rows = source[head * HEAD_DIM : (head + 1) * HEAD_DIM, :]
            for group in range(heads):
                piece = rows[:, group * HEAD_DIM : (group + 1) * HEAD_DIM]
                zero = jnp.zeros_like(piece)
                at, column = head * LANES, slice(group * LANES, (group + 1) * LANES)
                out_ref[index, at : at + HEAD_DIM, column] = jnp.concatenate([piece, zero], axis=1)
                out_ref[index, at + HEAD_DIM : at + LANES, column] = jnp.concatenate([zero, piece], axis=1)


def exchange(x, axis, bit):
    return lax.ppermute(x, axis, [(i, i ^ bit) for i in range(lax.axis_size(axis))])


def on_device(queries, keys, values, w_out):
    q, k, v = (jnp.transpose(x, (1, 0, 2)) for x in (queries, keys, values))
    heads, rows, _ = q.shape
    groups, count = lax.axis_size("head"), lax.axis_size("seq")
    params = pltpu.CompilerParams(vmem_limit_bytes=48 * 1024 * 1024)
    vk1, vk2, vk3, top, low_out, high_out = pl.pallas_call(
        prepare_kernel,
        grid=(heads,),
        in_specs=[head_block(rows, LANES)] * 2,
        out_specs=[
            head_block(rows, LANES),
            head_block(rows // 2, LANES),
            head_block(rows // 4, LANES),
            head_block(count, LANES),
            head_block(HALO_ROWS, LANES),
            head_block(HALO_ROWS, LANES),
        ],
        out_shape=[
            jax.ShapeDtypeStruct((heads, size, LANES), BF16)
            for size in (rows, rows // 2, rows // 4, count, HALO_ROWS, HALO_ROWS)
        ],
        scratch_shapes=[pltpu.VMEM((rows, LANES), F32)],
        compiler_params=params,
        name="prepare",
    )(k, v)
    low_in = lax.ppermute(high_out, "seq", ring(count, 1))
    high_in = lax.ppermute(low_out, "seq", ring(count, -1))
    me, width = lax.axis_index("head"), w_out.shape[1] // groups
    columns = [
        lax.dynamic_slice_in_dim(w_out, (me ^ bit) * width, width, axis=1) for bit in range(groups)
    ]
    columns = [x if bit == 0 else exchange(x, "head", bit) for bit, x in enumerate(columns)]
    w = pl.pallas_call(
        arrange_kernel,
        out_shape=jax.ShapeDtypeStruct((groups, heads * LANES, heads * LANES), BF16),
        compiler_params=params,
        name="arrange",
    )(*columns)
    tops = lax.all_to_all(top, "seq", split_axis=1, concat_axis=1, tiled=True)
    inner0, inner1 = 2 * rows - 2 * NR, rows - 2 * NR
    x0, m0, x1, m1 = pl.pallas_call(
        inner_kernel,
        grid=(heads,),
        in_specs=[head_block(rows, LANES)] * 4,
        out_specs=[head_block(size, LANES) for size in (inner0, inner0, inner1, inner1)],
        out_shape=[
            jax.ShapeDtypeStruct((heads, size, LANES), F32)
            for size in (inner0, inner0, inner1, inner1)
        ],
        scratch_shapes=[
            pltpu.VMEM((2 * rows, LANES), BF16),
            pltpu.VMEM((2 * rows, LANES), BF16),
            pltpu.VMEM((rows, LANES), F32),
        ],
        compiler_params=params,
        cost_estimate=pl.CostEstimate(flops=300_000_000, bytes_accessed=5_000_000, transcendentals=1_000_000),
        name="inner",
    )(q, k, v, vk1)
    place = lax.axis_index("seq").astype(jnp.int32).reshape(1)
    att = pl.pallas_call(
        outer_kernel,
        grid=(heads,),
        in_specs=[head_block(rows, LANES)] * 3
        + [head_block(size, LANES) for size in (rows, rows // 2, rows // 4, HALO_ROWS, HALO_ROWS, count)]
        + [head_block(size, LANES) for size in (inner0, inner0, inner1, inner1)]
        + [pl.BlockSpec(memory_space=pltpu.SMEM)],
        out_specs=head_block(rows, LANES),
        out_shape=jax.ShapeDtypeStruct((heads, rows, LANES), BF16),
        scratch_shapes=[
            pltpu.VMEM((6 * NR, LANES), BF16),
            pltpu.VMEM((6 * NR, LANES), BF16),
            pltpu.VMEM((rows + 2 * NR, LANES), BF16),
            pltpu.VMEM((rows // 2 + 2 * NR, LANES), BF16),
            pltpu.VMEM((rows // 4 + 2 * NR, LANES), BF16),
            pltpu.VMEM((2 * rows, LANES), BF16),
            pltpu.VMEM((rows, LANES), F32),
            pltpu.VMEM((2 * rows, LANES), F32),
            pltpu.VMEM((2 * rows, LANES), F32),
            pltpu.VMEM((2 * rows, LANES), F32),
            pltpu.VMEM((2 * rows, LANES), F32),
            pltpu.VMEM((rows, LANES), F32),
            pltpu.VMEM((rows, LANES), F32),
        ],
        compiler_params=params,
        name="outer",
    )(q, k, v, vk1, vk2, vk3, low_in, high_in, tops, x0, m0, x1, m1, place)
    sources = [att]
    bit = groups // 2
    while bit:
        sources = [x for pair in zip(sources, [exchange(x, "head", bit) for x in sources]) for x in pair]
        bit //= 2
    out = pl.pallas_call(
        project_kernel,
        out_shape=jax.ShapeDtypeStruct((heads, rows, LANES), BF16),
        compiler_params=params,
        name="project",
    )(*sources, w)
    return jnp.transpose(out, (1, 0, 2))


def solution(mesh):
    return jax.shard_map(
        on_device,
        mesh=mesh,
        in_specs=(
            P("seq", "head", None),
            P("seq", "head", None),
            P("seq", "head", None),
            P("head", None),
        ),
        out_specs=P("seq", "head", None),
        check_vma=False,
    )
```

```python
import functools
import math

import jax
import jax.numpy as jnp
from jax import lax
from jax.experimental import pallas as pl
from jax.experimental.pallas import tpu as pltpu
from jax.sharding import PartitionSpec as P

HEAD_DIM = 64
NR = 128
HALF = NR // 2
LANES = 2 * HEAD_DIM
LEVELS = 3
POOL = 1024
BF16 = jnp.bfloat16
F32 = jnp.float32
SCALE2 = HEAD_DIM ** (-0.5) * math.log2(math.e)
FAR = HALF
VMEM = 16 * 1024 * 1024
COST = 2500_000_000
HALO_ROWS = 2 * HALF + LEVELS * FAR


def low_lanes(rows):
    return lax.broadcasted_iota(jnp.int32, (rows, LANES), 1) < HEAD_DIM


def swap(x):
    return pltpu.roll(x, HEAD_DIM, 1)


def swap16(x):
    return pltpu.roll(x, HEAD_DIM, 1)


def fold_pairs(lo, hi):
    lo, hi = lo.astype(F32), hi.astype(F32)
    return jnp.where(low_lanes(lo.shape[0]), lo + swap(lo), hi + swap(hi))


def halve(scratch, x):
    rows = x.shape[0]
    scratch[pl.ds(0, rows), :] = x
    return scratch[pl.ds(0, rows // 2, 2), :] + scratch[pl.ds(1, rows // 2, 2), :]


def pooled_vk(sums, factor):
    scale = jnp.where(low_lanes(1), 1.0 / factor, factor ** (-0.5))
    return (sums * scale).astype(BF16)


def ones_high(v):
    return jnp.where(low_lanes(v.shape[0]), v, jnp.ones_like(v))


def put_pairs(keys, values, block, k, v):
    at = block * NR
    keys[at : at + HALF, :] = k
    keys[at + HALF : at + NR, :] = swap16(k)
    values[at : at + HALF, :] = ones_high(v)
    values[at + HALF : at + NR, :] = ones_high(swap16(v))


def put_pooled(keys, values, level, at, vk):
    lo, zero, size = low_lanes(vk.shape[0]), jnp.zeros_like(vk), vk.shape[0]
    keys[at : at + size, :] = jnp.where(lo, swap16(vk), zero) if level % 2 else jnp.where(lo, zero, vk)
    values[at : at + size, :] = ones_high(vk)


def kept_rows(window, half):
    at = (half // 2) * NR
    if half % 2 == 0:
        pieces = [(at, HALF), (at + 2 * NR, NR)]
    else:
        pieces = [(at, NR), (at + 2 * NR + HALF, HALF)]
    return [window[start : start + size, :] for start, size in pieces]


def scores_of(lhs, keys):
    return lax.dot_general(lhs, keys, (((1,), (1,)), ((), ())), preferred_element_type=F32)


def group_matrix(rows, shift):
    group = [lax.broadcasted_iota(jnp.int32, (rows, rows), axis) >> shift for axis in range(2)]
    return jnp.where(group[0] == group[1], 1.0, 0.0).astype(BF16)


def prepare_kernel(k_ref, v_ref, vk1, vk2, vk3, top, low_out, high_out, scratch):
    k, v = k_ref[0], v_ref[0]
    rows = k.shape[0]
    sums = fold_pairs(v, k)
    vk1[0] = pooled_vk(sums, 2)
    sums = halve(scratch, sums)
    vk2[0] = pooled_vk(sums, 4)
    sums = halve(scratch, sums)
    vk3[0] = pooled_vk(sums, 8)
    top[0] = jnp.broadcast_to(pooled_vk(jnp.sum(sums, axis=0, keepdims=True), POOL), top.shape[1:])
    for out, low in ((low_out, True), (high_out, False)):
        for index, source in enumerate((k_ref, v_ref, vk1, vk2, vk3)):
            near, count = (0 if index < 2 else HALF), source.shape[1]
            start = near if low else count - near - FAR
            out[0, index * FAR : (index + 1) * FAR, :] = source[0, start : start + FAR, :]


def coarse_kernel(q_ref, tops, q_top, tops_out):
    for head in range(q_ref.shape[0]):
        sums = jnp.sum(q_ref[head].astype(F32), axis=0, keepdims=True)
        q_top[head] = jnp.broadcast_to((sums + swap(sums)) * POOL ** (-0.5), q_top.shape[1:])
        tops_out[head] = tops[head]


def attend_kernel(
    q_ref, k_ref, v_ref, vk1, vk2, vk3, low_in, high_in, top_query, top, place, att,
    keys0, values0, keys1, values1, keys2, values2, keys3, values3, scratch,
):
    rows = q_ref.shape[1]
    blocks = rows // HALF
    def low_halo(index):
        return low_in[0, index * FAR : (index + 1) * FAR, :]

    def high_halo(index):
        at = slice(index * FAR, (index + 1) * FAR)
        return high_in[0, at, :]

    put_pairs(keys0, values0, 0, low_halo(0), low_halo(1))
    put_pairs(keys0, values0, blocks + 1, high_halo(0), high_halo(1))
    for block in range(blocks):
        at = slice(block * HALF, (block + 1) * HALF)
        put_pairs(keys0, values0, block + 1, k_ref[0, at, :], v_ref[0, at, :])
    pooled = ((keys1, values1, vk1), (keys2, values2, vk2), (keys3, values3, vk3))
    for level, (keys, values, own) in enumerate(pooled, 1):
        put_pooled(keys, values, level, NR, own[0])
    for low in (True, False):
        halo = low_halo if low else high_halo
        sums = fold_pairs(halo(1), halo(0))
        for level, (keys, values, own) in enumerate(pooled, 1):
            count = own.shape[1]
            if level > 1:
                sums = halve(scratch, jnp.concatenate([beyond, sums] if low else [sums, beyond], axis=0))
            far = halo(level + 1)
            put_pooled(keys, values, level, FAR if low else NR + count, pooled_vk(sums, 2**level))
            put_pooled(keys, values, level, 0 if low else NR + count + FAR, far)
            beyond = far.astype(F32) * jnp.where(low_lanes(1), 2.0**level, 2.0 ** (level / 2))
    positions = top.shape[1]
    top_keys = jnp.where(low_lanes(positions), jnp.zeros_like(top[0]), top[0])
    top_values = ones_high(top[0])
    q_top = top_query[0, 0:1, :]
    lane = lax.broadcasted_iota(jnp.int32, (HALF, LANES), 1)
    distance = lane - HEAD_DIM - place[0]
    distance = jnp.where(distance < 0, distance + positions, distance)
    keep = (lane < HEAD_DIM) | ((distance >= 2) & (distance <= positions - 2))
    lo = low_lanes(HALF)
    pairs, fours = group_matrix(HALF, 1), group_matrix(HALF, 2)

    def pooled_queries(block):
        q = q_ref[0, block * HALF : (block + 1) * HALF, :]
        zero = jnp.zeros_like(q)
        lhs = jnp.concatenate([jnp.where(lo, q, zero), jnp.where(lo, swap16(q), zero)], axis=0)
        q1, q2, q3 = (
            (sums + swap(sums)) * factor ** (-0.5)
            for sums, factor in (
                (q.astype(F32), 2),
                (jnp.dot(pairs, q, preferred_element_type=F32), 4),
                (jnp.dot(fours, q, preferred_element_type=F32), 8),
            )
        )
        lhs12 = jnp.where(lo, q1, q2).astype(BF16)
        lhs3t = jnp.where(lo, q3, q_top).astype(BF16)
        return lhs, lhs12, lhs3t

    def scores(block, lhs, lhs12, lhs3t):
        halves = (block, block // 2, block // 4)
        s0 = scores_of(lhs, keys0[block * NR : (block + 3) * NR, :])
        s12 = scores_of(lhs12, jnp.concatenate(kept_rows(keys1, halves[0]) + kept_rows(keys2, halves[1]), axis=0))
        s3t = scores_of(lhs3t, jnp.concatenate(kept_rows(keys3, halves[2]) + [top_keys], axis=0))
        return s0, s12, s3t

    def weights(block, s0, s12, s3t):
        masked = jnp.where(keep, s3t[:, LANES:], -jnp.inf)
        su = jnp.concatenate([s12, s3t[:, :LANES], masked], axis=1)
        mu = jnp.max(su, axis=1, keepdims=True)
        m0 = jnp.max(s0, axis=1, keepdims=True)
        pu = jnp.exp2((su - mu) * SCALE2).astype(BF16)
        mu = jnp.concatenate([mu, mu], axis=0)
        m = jnp.maximum(m0, mu)
        p0 = jnp.exp2((s0 - m) * SCALE2).astype(BF16)
        return p0, pu, jnp.exp2((mu - m) * SCALE2)

    def products(block, p0, pu, share):
        halves = (block, block // 2, block // 4)
        values = kept_rows(values1, halves[0]) + kept_rows(values2, halves[1]) + kept_rows(values3, halves[2])
        xu = jnp.dot(pu, jnp.concatenate(values + [top_values], axis=0), preferred_element_type=F32)
        x0 = jnp.dot(p0, values0[block * NR : (block + 3) * NR, :], preferred_element_type=F32)
        return x0, xu, share

    def finish(block, x0, xu, share):
        x = x0 + jnp.concatenate([xu, xu], axis=0) * share
        x = x / swap(x)
        out = jnp.where(lo, x[:HALF], swap(x[HALF:]))
        att[0, block * HALF : (block + 1) * HALF, :] = out.astype(BF16)

    stages = (pooled_queries, scores, weights, products, finish)
    held = [{} for _ in stages]
    for step in range(blocks + len(stages) - 1):
        for index in range(len(stages)):
            block = step - index
            if 0 <= block < blocks:
                given = held[index - 1].pop(block) if index else ()
                held[index][block] = stages[index](block, *given)


def pair_weights(source, head, group):
    piece = source[head * HEAD_DIM : (head + 1) * HEAD_DIM, group * HEAD_DIM : (group + 1) * HEAD_DIM]
    zero = jnp.zeros_like(piece)
    return jnp.concatenate(
        [jnp.concatenate([piece, zero], axis=1), jnp.concatenate([zero, piece], axis=1)], axis=0
    )


def project_kernel(terms, *refs):
    *inputs, out_ref = refs
    groups, heads = len({source for source, _ in terms}), out_ref.shape[0]
    att, inputs = inputs[: len(terms)], inputs[len(terms) :]
    w = dict(zip(sorted({source for source, _ in terms}), inputs))
    rows = jnp.concatenate([ref[...] for ref in att], axis=1)
    for group in range(heads):
        columns = jnp.concatenate([pair_weights(w[source][...], head, group) for source, head in terms], axis=0)
        total = jnp.dot(rows, columns, preferred_element_type=F32)
        if len(inputs) > groups:
            total = total + inputs[groups][group]
        out_ref[group] = total.astype(out_ref.dtype)


def head_block(*shape):
    return pl.BlockSpec((1,) + shape, lambda h: (h,) + (0,) * len(shape))


def ring(count, step):
    return [(i, (i + step) % count) for i in range(count)]


def exchange(x, axis, bit):
    return lax.ppermute(x, axis, [(i, i ^ bit) for i in range(lax.axis_size(axis))])


def on_device(queries, keys, values, w_out):
    q, k, v = (jnp.transpose(x, (1, 0, 2)) for x in (queries, keys, values))
    heads, rows, _ = q.shape
    groups, count = lax.axis_size("head"), lax.axis_size("seq")
    params = pltpu.CompilerParams(vmem_limit_bytes=62 * 1024 * 1024)
    vk1, vk2, vk3, top, low_out, high_out = pl.pallas_call(
        prepare_kernel,
        grid=(heads,),
        in_specs=[head_block(rows, LANES)] * 2,
        out_specs=[
            head_block(rows, LANES),
            head_block(rows // 2, LANES),
            head_block(rows // 4, LANES),
            head_block(count, LANES),
            head_block(HALO_ROWS, LANES),
            head_block(HALO_ROWS, LANES),
        ],
        out_shape=[
            jax.ShapeDtypeStruct((heads, size, LANES), BF16)
            for size in (rows, rows // 2, rows // 4, count, HALO_ROWS, HALO_ROWS)
        ],
        scratch_shapes=[pltpu.VMEM((rows, LANES), F32)],
        compiler_params=params,
        name="prepare",
    )(k, v)
    low_in = lax.ppermute(high_out, "seq", ring(count, 1))
    high_in = lax.ppermute(low_out, "seq", ring(count, -1))
    me, width = lax.axis_index("head"), w_out.shape[1] // groups
    top, w_out = lax.optimization_barrier((top, w_out))

    def columns_of(index):
        return lax.dynamic_slice_in_dim(w_out, index * width, width, axis=1)

    columns = [columns_of(me)]
    if groups > 2:
        near = exchange(jnp.stack([columns_of(me ^ 1), columns_of(me ^ 3)]), "head", 1)
        far = exchange(jnp.stack([columns_of(me ^ 2), near[1]]), "head", 2)
        columns += [near[0], far[0], far[1]]
    elif groups > 1:
        columns += [exchange(columns_of(me ^ 1), "head", 1)]
    tops = lax.all_to_all(top, "seq", split_axis=1, concat_axis=1, tiled=True)
    top_queries, tops = pl.pallas_call(
        coarse_kernel,
        out_shape=[
            jax.ShapeDtypeStruct((heads, 8, LANES), F32),
            jax.ShapeDtypeStruct((heads, count, LANES), BF16),
        ],
        compiler_params=pltpu.CompilerParams(vmem_limit_bytes=VMEM),
        cost_estimate=pl.CostEstimate(flops=COST, bytes_accessed=1_000_000, transcendentals=0),
        name="coarse",
    )(q, tops)
    place = lax.axis_index("seq").astype(jnp.int32).reshape(1)
    sizes = [2 * rows + 2 * NR] + [(rows >> level) + 2 * NR for level in range(LEVELS)]
    bits = [bit for bit in (2, 1) if bit < groups]
    sources = [[] for _ in range(groups)]
    for head in range(heads):
        def one_head(size, head=head):
            return pl.BlockSpec((1, size, LANES), lambda i: (head, 0, 0))

        att = pl.pallas_call(
            attend_kernel,
            grid=(1,),
            in_specs=[one_head(rows)] * 3
            + [one_head(size) for size in (rows, rows // 2, rows // 4, HALO_ROWS, HALO_ROWS)]
            + [one_head(8), one_head(count)]
            + [pl.BlockSpec(memory_space=pltpu.SMEM)],
            out_specs=pl.BlockSpec((1, rows, LANES), lambda i: (0, 0, 0)),
            out_shape=jax.ShapeDtypeStruct((1, rows, LANES), BF16),
            scratch_shapes=[pltpu.VMEM((size, LANES), BF16) for size in sizes for _ in range(2)]
            + [pltpu.VMEM((rows, LANES), F32)],
            compiler_params=pltpu.CompilerParams(vmem_limit_bytes=VMEM),
            name=f"attend{head}",
        )(q, k, v, vk1, vk2, vk3, low_in, high_in, top_queries, tops, place)[0]
        parts = {0: att}
        for bit in bits:
            parts.update({index ^ bit: exchange(x, "head", bit) for index, x in parts.items()})
        for index, x in parts.items():
            sources[index].append(x)
    order = [(source, head) for source in range(groups) for head in range(heads)]
    late = [term for term in order if term[1] == heads - 1 and term[0] & 2]
    early = [term for term in order if term not in late]
    out = []
    for terms, dtype in ((early, F32), (late, BF16)):
        if terms:
            out = [
                pl.pallas_call(
                    functools.partial(project_kernel, terms),
                    out_shape=jax.ShapeDtypeStruct((heads, rows, LANES), dtype if late else BF16),
                    compiler_params=pltpu.CompilerParams(vmem_limit_bytes=VMEM),
                    name="project",
                )(*[sources[source][head] for source, head in terms], *[columns[source] for source in sorted({source for source, _ in terms})], *out)
            ]
    out = out[0]
    return jnp.transpose(out, (1, 0, 2))


def solution(mesh):
    return jax.shard_map(
        on_device,
        mesh=mesh,
        in_specs=(
            P("seq", "head", None),
            P("seq", "head", None),
            P("seq", "head", None),
            P("head", None),
        ),
        out_specs=P("seq", "head", None),
        check_vma=False,
    )
```

```python
import functools
import math

import jax
import jax.numpy as jnp
from jax import lax
from jax.experimental import pallas as pl
from jax.experimental.pallas import tpu as pltpu
from jax.sharding import PartitionSpec as P

HEAD_DIM = 64
NR = 128
HALF = NR // 2
LANES = 2 * HEAD_DIM
LEVELS = 3
POOL = 1024
BF16 = jnp.bfloat16
F32 = jnp.float32
SCALE2 = HEAD_DIM ** (-0.5) * math.log2(math.e)
FAR = HALF
VMEM = 16 * 1024 * 1024
LAST = 2
HALO_ROWS = 2 * HALF + LEVELS * FAR


def low_lanes(rows):
    return lax.broadcasted_iota(jnp.int32, (rows, LANES), 1) < HEAD_DIM


def swap(x):
    return pltpu.roll(x, HEAD_DIM, 1)


def swap16(x):
    return pltpu.roll(x, HEAD_DIM, 1)


def fold_pairs(lo, hi):
    lo, hi = lo.astype(F32), hi.astype(F32)
    return jnp.where(low_lanes(lo.shape[0]), lo + swap(lo), hi + swap(hi))


def halve(scratch, x):
    rows = x.shape[0]
    scratch[pl.ds(0, rows), :] = x
    return scratch[pl.ds(0, rows // 2, 2), :] + scratch[pl.ds(1, rows // 2, 2), :]


def pooled_vk(sums, factor):
    scale = jnp.where(low_lanes(1), 1.0 / factor, factor ** (-0.5))
    return (sums * scale).astype(BF16)


def ones_high(v):
    return jnp.where(low_lanes(v.shape[0]), v, jnp.ones_like(v))


def put_pairs(keys, values, block, k, v):
    at = block * NR
    keys[at : at + HALF, :] = k
    keys[at + HALF : at + NR, :] = swap16(k)
    values[at : at + HALF, :] = ones_high(v)
    values[at + HALF : at + NR, :] = ones_high(swap16(v))


def put_pooled(keys, values, level, at, vk):
    lo, zero, size = low_lanes(vk.shape[0]), jnp.zeros_like(vk), vk.shape[0]
    keys[at : at + size, :] = jnp.where(lo, swap16(vk), zero) if level % 2 else jnp.where(lo, zero, vk)
    values[at : at + size, :] = ones_high(vk)


def scores_of(lhs, keys):
    return lax.dot_general(lhs, keys, (((1,), (1,)), ((), ())), preferred_element_type=F32)


def group_matrix(rows, shift):
    group = [lax.broadcasted_iota(jnp.int32, (rows, rows), axis) >> shift for axis in range(2)]
    return jnp.where(group[0] == group[1], 1.0, 0.0).astype(BF16)


def prepare_kernel(k, v, top, low_out, high_out, scratch):
    heads, rows = k.shape[0], k.shape[1]
    for head in range(heads):
        for out, at in ((low_out, 0), (high_out, rows - HALF)):
            for index, source in enumerate((k, v)):
                out[head, index * FAR : (index + 1) * FAR, :] = source[head, at : at + HALF, :]
        sums = fold_pairs(v[head], k[head])
        for level in range(1, LEVELS + 1):
            if level > 1:
                sums = halve(scratch.at[head], sums)
            vk, at = pooled_vk(sums, 2**level), (level + 1) * FAR
            low_out[head, at : at + FAR, :] = vk[HALF : HALF + FAR]
            high_out[head, at : at + FAR, :] = vk[vk.shape[0] - HALF - FAR : vk.shape[0] - HALF]
        top[head] = jnp.broadcast_to(pooled_vk(jnp.sum(sums, axis=0, keepdims=True), POOL), top.shape[1:])


def cut_kernel(w_ref, me, *outs):
    half, width = outs[0].shape[1], w_ref.shape[1] // me.shape[1]
    for index in range(me.shape[1]):

        @pl.when(me[0, 0] == index)
        def _(index=index):
            for slot, out in enumerate(outs):
                for core in range(2):
                    at = (index ^ (2 * slot + core)) * width
                    out[:, core * width : (core + 1) * width] = w_ref[:, at : at + width]


def coarse_kernel(tops, keys, values):
    for head in range(tops.shape[0]):
        keys[head] = jnp.where(low_lanes(tops.shape[1]), jnp.zeros_like(tops[head]), tops[head])
        values[head] = ones_high(tops[head])


def run_stages(stages, blocks):
    held = [{} for _ in stages]
    for step in range(len(blocks) + len(stages) - 1):
        for index, stage in enumerate(stages):
            at = step - index
            if 0 <= at < len(blocks):
                given = held[index - 1].pop(at) if index else ()
                held[index][at] = stage(blocks[at], *given)


def token_queries(q):
    lo, zero = low_lanes(q.shape[0]), jnp.zeros_like(q)
    return jnp.concatenate([jnp.where(lo, q, zero), jnp.where(lo, swap16(q), zero)], axis=0)


def inner_kernel(q_ref, k_ref, v_ref, x0, m0, lhs12, lhs3t, *rest):
    own, (keys0, values0, scratch) = rest[:-3], rest[-3:]
    heads, rows = q_ref.shape[0], q_ref.shape[1]
    blocks = rows // HALF
    lo = low_lanes(HALF)
    pairs, fours = group_matrix(HALF, 1), group_matrix(HALF, 2)

    def one_head(head, _):
        for block in range(blocks):
            at = slice(block * HALF, (block + 1) * HALF)
            put_pairs(keys0, values0, block, k_ref[head, at, :], v_ref[head, at, :])
        q_top = jnp.sum(q_ref[head].astype(F32), axis=0, keepdims=True)
        q_top = (q_top + swap(q_top)) * POOL ** (-0.5)

        def scores(block):
            q = q_ref[head, block * HALF : (block + 1) * HALF, :]
            return (scores_of(token_queries(q), keys0[(block - 1) * NR : (block + 2) * NR, :]),)

        def weights(block, s0):
            m = jnp.max(s0, axis=1, keepdims=True)
            return m, jnp.exp2((s0 - m) * SCALE2).astype(BF16)

        def products(block, m, p0):
            at = slice((block - 1) * NR, block * NR)
            x0[head, at, :] = jnp.dot(p0, values0[(block - 1) * NR : (block + 2) * NR, :], preferred_element_type=F32)
            m0[head, at, :] = jnp.broadcast_to(m, (NR, LANES))

        run_stages((scores, weights, products), range(1, blocks - 1))
        for block in range(blocks):
            at = slice(block * HALF, (block + 1) * HALF)
            q = q_ref[head, at, :]
            q1, q2, q3 = (
                (sums + swap(sums)) * factor ** (-0.5)
                for sums, factor in (
                    (q.astype(F32), 2),
                    (jnp.dot(pairs, q, preferred_element_type=F32), 4),
                    (jnp.dot(fours, q, preferred_element_type=F32), 8),
                )
            )
            lhs12[head, at, :] = jnp.where(lo, q1, q2).astype(BF16)
            lhs3t[head, at, :] = jnp.where(lo, q3, q_top).astype(BF16)
        sums = fold_pairs(v_ref[head], k_ref[head])
        for level in range(1, LEVELS + 1):
            if level > 1:
                sums = halve(scratch, sums)
            put_pooled(own[2 * level - 2].at[head], own[2 * level - 1].at[head], level, 0, pooled_vk(sums, 2**level))
        return 0

    lax.fori_loop(0, heads, one_head, 0)


def attend_kernel(head, q_ref, k_ref, v_ref, x0_in, m0_in, lhs12, lhs3t, *rest):
    own, rest = rest[:6], rest[6:]
    low_in, high_in, top_keys_in, top_values_in, place, att, keys0, values0, halo_keys, halo_values, scratch = rest
    rows = q_ref.shape[1]
    blocks = rows // HALF
    for low in (True, False):
        source = low_in if low else high_in

        def halo(index):
            return source[head, index * FAR : (index + 1) * FAR, :]

        sums = fold_pairs(halo(1), halo(0))
        for level in range(1, LEVELS + 1):
            if level > 1:
                sums = halve(scratch, jnp.concatenate([beyond, sums] if low else [sums, beyond], axis=0))
            far = halo(level + 1)
            base = (2 * level - 2 + (not low)) * NR
            put_pooled(halo_keys, halo_values, level, base + (FAR if low else 0), pooled_vk(sums, 2**level))
            put_pooled(halo_keys, halo_values, level, base + (0 if low else FAR), far)
            beyond = far.astype(F32) * jnp.where(low_lanes(1), 2.0**level, 2.0 ** (level / 2))
        k, v = halo(0), halo(1)
        first = 0 if low else 3
        if low:
            put_pairs(keys0, values0, 0, k, v)
        else:
            put_pairs(keys0, values0, 5, k, v)
        for index in range(2):
            at = slice(index * HALF, (index + 1) * HALF) if low else slice(rows - (2 - index) * HALF, rows - (1 - index) * HALF)
            put_pairs(keys0, values0, first + index + (1 if low else 0), k_ref[head, at, :], v_ref[head, at, :])

    def kept(level, half, which):
        mine, halo = own[2 * level - 2 + which], (halo_keys, halo_values)[which]
        count, at = mine.shape[1], (half // 2) * NR - NR
        spans = [(at, HALF), (at + 2 * NR, NR)] if half % 2 == 0 else [(at, NR), (at + 2 * NR + HALF, HALF)]
        pieces = []
        for start, size in spans:
            if start < 0:
                start += (2 * level - 1) * NR
                pieces.append(halo[start : start + size, :])
            elif start >= count:
                start += (2 * level - 1) * NR - count
                pieces.append(halo[start : start + size, :])
            else:
                pieces.append(mine[head, start : start + size, :])
        return pieces

    positions = top_keys_in.shape[1]
    top_keys, top_values = top_keys_in[head], top_values_in[head]
    lane = lax.broadcasted_iota(jnp.int32, (HALF, LANES), 1)
    distance = lane - HEAD_DIM - place[0]
    distance = jnp.where(distance < 0, distance + positions, distance)
    keep = (lane < HEAD_DIM) | ((distance >= 2) & (distance <= positions - 2))
    lo = low_lanes(HALF)

    def edge_window(block):
        return slice(0, 3 * NR) if block == 0 else slice(3 * NR, 6 * NR)

    def scores(block):
        at = slice(block * HALF, (block + 1) * HALF)
        s12 = scores_of(lhs12[head, at, :], jnp.concatenate(kept(1, block, 0) + kept(2, block // 2, 0), axis=0))
        s3t = scores_of(lhs3t[head, at, :], jnp.concatenate(kept(3, block // 4, 0) + [top_keys], axis=0))
        s0 = None
        if block in (0, blocks - 1):
            s0 = scores_of(token_queries(q_ref[head, at, :]), keys0[edge_window(block), :])
        return s0, s12, s3t

    def weights(block, s0, s12, s3t):
        masked = jnp.where(keep, s3t[:, LANES:], -jnp.inf)
        su = jnp.concatenate([s12, s3t[:, :LANES], masked], axis=1)
        mu = jnp.max(su, axis=1, keepdims=True)
        pu = jnp.exp2((su - mu) * SCALE2).astype(BF16)
        mu = jnp.concatenate([mu, mu], axis=0)
        if s0 is None:
            m0 = m0_in[head, (block - 1) * NR : block * NR, :]
            m = jnp.maximum(m0, mu)
            return None, jnp.exp2((m0 - m) * SCALE2), pu, jnp.exp2((mu - m) * SCALE2)
        m = jnp.maximum(jnp.max(s0, axis=1, keepdims=True), mu)
        return jnp.exp2((s0 - m) * SCALE2).astype(BF16), None, pu, jnp.exp2((mu - m) * SCALE2)

    def products(block, p0, share0, pu, share):
        values = kept(1, block, 1) + kept(2, block // 2, 1) + kept(3, block // 4, 1)
        xu = jnp.dot(pu, jnp.concatenate(values + [top_values], axis=0), preferred_element_type=F32)
        if p0 is None:
            x = x0_in[head, (block - 1) * NR : block * NR, :] * share0
        else:
            x = jnp.dot(p0, values0[edge_window(block), :], preferred_element_type=F32)
        return x, xu, share

    def finish(block, x, xu, share):
        x = x + jnp.concatenate([xu, xu], axis=0) * share
        x = x / swap(x)
        out = jnp.where(lo, x[:HALF], swap(x[HALF:]))
        att[0, block * HALF : (block + 1) * HALF, :] = out.astype(BF16)

    run_stages((scores, weights, products, finish), range(blocks))


def pair_weights(source, head, group):
    piece = source[head * HEAD_DIM : (head + 1) * HEAD_DIM, group * HEAD_DIM : (group + 1) * HEAD_DIM]
    zero = jnp.zeros_like(piece)
    return jnp.concatenate(
        [jnp.concatenate([piece, zero], axis=1), jnp.concatenate([zero, piece], axis=1)], axis=0
    )


def project_kernel(terms, *refs):
    count = len(terms)
    att, w, rest = refs[:count], refs[count : count + 2], refs[count + 2 :]
    earlier, outs = (rest[:2], rest[2:]) if len(rest) > 2 else (None, rest)
    heads = outs[0].shape[0]
    rows = jnp.concatenate([ref[...] for ref in att], axis=1)
    for core, out in enumerate(outs):
        for group in range(heads):
            columns = [pair_weights(w[source][...], head, core * heads + group) for source, head in terms]
            total = jnp.dot(rows, jnp.concatenate(columns, axis=0), preferred_element_type=F32)
            if earlier:
                total = total + earlier[core][group]
            out[group] = total.astype(out.dtype)


def add_kernel(mine, other, out):
    out[...] = (mine[...] + other[...].astype(F32)).astype(BF16)


def ring(count, step):
    return [(i, (i + step) % count) for i in range(count)]


def exchange(x, axis, bit):
    return lax.ppermute(x, axis, [(i, i ^ bit) for i in range(lax.axis_size(axis))])


def on_device(queries, keys, values, w_out):
    q, k, v = (jnp.transpose(x, (1, 0, 2)) for x in (queries, keys, values))
    heads, rows, _ = q.shape
    groups, count = lax.axis_size("head"), lax.axis_size("seq")
    params = pltpu.CompilerParams(vmem_limit_bytes=VMEM)
    vmem = pl.BlockSpec(memory_space=pltpu.VMEM)

    def shape(size, dtype=BF16):
        return jax.ShapeDtypeStruct((heads, size, LANES), dtype)

    messages = (count, HALO_ROWS, HALO_ROWS)
    top, low_out, high_out = pl.pallas_call(
        prepare_kernel,
        in_specs=[vmem] * 2,
        out_specs=[vmem] * 3,
        out_shape=[shape(size) for size in messages],
        scratch_shapes=[pltpu.VMEM((heads, rows, LANES), F32)],
        compiler_params=params,
        name="prepare",
    )(k, v)
    low_in = lax.ppermute(high_out, "seq", ring(count, 1))
    high_in = lax.ppermute(low_out, "seq", ring(count, -1))
    tops = lax.all_to_all(top, "seq", split_axis=1, concat_axis=1, tiled=True)
    top_keys, top_values = pl.pallas_call(
        coarse_kernel,
        in_specs=[vmem],
        out_specs=[vmem] * 2,
        out_shape=[shape(count)] * 2,
        compiler_params=params,
        name="coarse",
    )(tops)
    top, w_out = lax.optimization_barrier((top, w_out))
    width = w_out.shape[1] // groups
    me = jnp.full((1, groups), lax.axis_index("head"), jnp.int32)
    w_own, w_far = pl.pallas_call(
        cut_kernel,
        in_specs=[vmem, pl.BlockSpec(memory_space=pltpu.SMEM)],
        out_shape=[jax.ShapeDtypeStruct((w_out.shape[0], 2 * width), BF16)] * 2,
        compiler_params=params,
        name="cut",
    )(w_out, me)
    w_far = exchange(w_far, "head", 2)

    top_keys, q = lax.optimization_barrier((top_keys, q))
    pooled = [rows >> level for level in range(LEVELS) for _ in range(2)]
    inner = pl.pallas_call(
        inner_kernel,
        in_specs=[vmem] * 3,
        out_specs=[vmem] * 10,
        out_shape=[shape(2 * rows - 2 * NR, F32)] * 2 + [shape(rows)] * 2 + [shape(size) for size in pooled],
        scratch_shapes=[pltpu.VMEM((2 * rows, LANES), BF16)] * 2 + [pltpu.VMEM((rows, LANES), F32)],
        compiler_params=params,
        cost_estimate=pl.CostEstimate(flops=4_000_000_000, bytes_accessed=8_000_000, transcendentals=1_000_000),
        name="inner",
    )(q, k, v)
    place = lax.axis_index("seq").astype(jnp.int32).reshape(1)
    parts = {}
    for head in range(heads):
        att = pl.pallas_call(
            functools.partial(attend_kernel, head),
            in_specs=[vmem] * 17 + [pl.BlockSpec(memory_space=pltpu.SMEM)],
            out_shape=jax.ShapeDtypeStruct((1, rows, LANES), BF16),
            scratch_shapes=[pltpu.VMEM((6 * NR, LANES), BF16)] * 4 + [pltpu.VMEM((NR, LANES), F32)],
            compiler_params=params,
            name=f"attend{head}",
        )(q, k, v, *inner, low_in, high_in, top_keys, top_values, place)[0]
        parts[0, head], parts[1, head] = att, exchange(att, "head", 2)
    late = [(1, LAST)]
    early = [term for term in parts if term not in late]
    shares = []
    for terms, types in ((early, (F32, F32)), (late, (F32, BF16))):
        shares = pl.pallas_call(
            functools.partial(project_kernel, terms),
            in_specs=[vmem] * (len(terms) + 2 + len(shares)),
            out_specs=[vmem] * 2,
            out_shape=[shape(rows, dtype) for dtype in types],
            compiler_params=params,
            name="project",
        )(*[parts[term] for term in terms], w_own, w_far, *shares)
    out = pl.pallas_call(
        add_kernel,
        grid=(heads,),
        in_specs=[pl.BlockSpec((1, rows, LANES), lambda h: (h, 0, 0))] * 2,
        out_specs=pl.BlockSpec((1, rows, LANES), lambda h: (h, 0, 0)),
        out_shape=shape(rows),
        compiler_params=params,
        name="add",
    )(shares[0], exchange(shares[1], "head", 1))
    return jnp.transpose(out, (1, 0, 2))


def solution(mesh):
    return jax.shard_map(
        on_device,
        mesh=mesh,
        in_specs=(
            P("seq", "head", None),
            P("seq", "head", None),
            P("seq", "head", None),
            P("head", None),
        ),
        out_specs=P("seq", "head", None),
        check_vma=False,
    )
```

```python
import functools
import math

import jax
import jax.numpy as jnp
from jax import lax
from jax.experimental import pallas as pl
from jax.experimental.pallas import tpu as pltpu
from jax.sharding import PartitionSpec as P

HEAD_DIM = 64
NR = 128
HALF = NR // 2
LANES = 2 * HEAD_DIM
LEVELS = 3
POOL = 1024
BF16 = jnp.bfloat16
F32 = jnp.float32
SCALE2 = HEAD_DIM ** (-0.5) * math.log2(math.e)
FAR = HALF
VMEM = 16 * 1024 * 1024
LAST = 2
HALO_ROWS = 2 * HALF + LEVELS * FAR


def low_lanes(rows):
    return lax.broadcasted_iota(jnp.int32, (rows, LANES), 1) < HEAD_DIM


def swap(x):
    return pltpu.roll(x, HEAD_DIM, 1)


def swap16(x):
    return pltpu.roll(x, HEAD_DIM, 1)


def fold_pairs(lo, hi):
    lo, hi = lo.astype(F32), hi.astype(F32)
    return jnp.where(low_lanes(lo.shape[0]), lo + swap(lo), hi + swap(hi))


def halve(scratch, x):
    rows = x.shape[0]
    scratch[pl.ds(0, rows), :] = x
    return scratch[pl.ds(0, rows // 2, 2), :] + scratch[pl.ds(1, rows // 2, 2), :]


def pooled_vk(sums, factor):
    scale = jnp.where(low_lanes(1), 1.0 / factor, factor ** (-0.5))
    return (sums * scale).astype(BF16)


def ones_high(v):
    return jnp.where(low_lanes(v.shape[0]), v, jnp.ones_like(v))


def put_pairs(keys, values, block, k, v):
    at = block * NR
    keys[at : at + HALF, :] = k
    keys[at + HALF : at + NR, :] = swap16(k)
    values[at : at + HALF, :] = ones_high(v)
    values[at + HALF : at + NR, :] = ones_high(swap16(v))


def scores_of(lhs, keys):
    return lax.dot_general(lhs, keys, (((1,), (1,)), ((), ())), preferred_element_type=F32)


def group_matrix(rows, shift):
    group = [lax.broadcasted_iota(jnp.int32, (rows, rows), axis) >> shift for axis in range(2)]
    return jnp.where(group[0] == group[1], 1.0, 0.0).astype(BF16)


def prepare_kernel(k_hbm, v_hbm, place, top, first_out, second_out, k, v, scratch, read):
    heads, rows = k.shape[0], k.shape[1]
    even = lax.rem(place[0], 2) == 0
    loads = [
        [
            pltpu.make_async_copy(source.at[head], into.at[head], read.at[head, index])
            for index, (source, into) in enumerate(((k_hbm, k), (v_hbm, v)))
        ]
        for head in range(heads)
    ]
    for pair in loads:
        for copy in pair:
            copy.start()
    for head in range(heads):
        for copy in loads[head]:
            copy.wait()
        lows, highs = [], []
        for source in (k, v):
            lows.append(source[head, 0:HALF, :])
            highs.append(source[head, rows - HALF : rows, :])
        sums = fold_pairs(v[head], k[head])
        for level in range(1, LEVELS + 1):
            if level > 1:
                sums = halve(scratch.at[head], sums)
            vk = pooled_vk(sums, 2**level)
            lows.append(vk[HALF : HALF + FAR])
            highs.append(vk[vk.shape[0] - HALF - FAR : vk.shape[0] - HALF])
        for index, (low, high) in enumerate(zip(lows, highs)):
            at = slice(index * FAR, (index + 1) * FAR)
            first_out[head, at, :] = jnp.where(even, high, low)
            second_out[head, at, :] = jnp.where(even, low, high)
        top[:, head, :] = jnp.broadcast_to(pooled_vk(jnp.sum(sums, axis=0, keepdims=True), POOL), (top.shape[0], LANES))


def cut_kernel(w_ref, me, *outs):
    half, width = outs[0].shape[1], w_ref.shape[1] // me.shape[1]
    for index in range(me.shape[1]):

        @pl.when(me[0, 0] == index)
        def _(index=index):
            for slot, out in enumerate(outs):
                for core in range(2):
                    at = (index ^ (2 * slot + core)) * width
                    out[:, core * width : (core + 1) * width] = w_ref[:, at : at + width]


def run_stages(stages, blocks):
    held = [{} for _ in stages]
    for step in range(len(blocks) + len(stages) - 1):
        for index, stage in enumerate(stages):
            at = step - index
            if 0 <= at < len(blocks):
                given = held[index - 1].pop(at) if index else ()
                held[index][at] = stage(blocks[at], *given)


def token_queries(q):
    lo, zero = low_lanes(q.shape[0]), jnp.zeros_like(q)
    return jnp.concatenate([jnp.where(lo, q, zero), jnp.where(lo, swap16(q), zero)], axis=0)


def inner_kernel(q_ref, k_ref, v_ref, x0, m0, lhs12, lhs3t, vk1, vk2, vk3, keys0, values0, scratch):
    heads, rows = q_ref.shape[0], q_ref.shape[1]
    blocks = rows // HALF
    lo = low_lanes(HALF)
    pairs, fours = group_matrix(HALF, 1), group_matrix(HALF, 2)

    def one_head(head, _):
        for block in range(blocks):
            at = slice(block * HALF, (block + 1) * HALF)
            put_pairs(keys0, values0, block, k_ref[head, at, :], v_ref[head, at, :])
        wide = jnp.concatenate([q_ref[head, block * HALF : (block + 1) * HALF, :] for block in range(blocks)], axis=1)
        wide2 = jnp.dot(pairs, wide, preferred_element_type=F32)
        wide3 = jnp.dot(fours, wide, preferred_element_type=F32)
        q_top = jnp.sum(q_ref[head].astype(F32), axis=0, keepdims=True)
        q_top = (q_top + swap(q_top)) * POOL ** (-0.5)

        def queries(block):
            at, lanes = slice(block * HALF, (block + 1) * HALF), slice(block * LANES, (block + 1) * LANES)
            q1, q2, q3 = (
                (sums + swap(sums)) * factor ** (-0.5)
                for sums, factor in ((q_ref[head, at, :].astype(F32), 2), (wide2[:, lanes], 4), (wide3[:, lanes], 8))
            )
            lhs12[head, at, :] = jnp.where(lo, q2, q1).astype(BF16)
            lhs3t[head, at, :] = jnp.where(lo, q_top, q3).astype(BF16)

        def scores(block):
            queries(block)
            if block in (0, blocks - 1):
                return (None,)
            q = q_ref[head, block * HALF : (block + 1) * HALF, :]
            return (scores_of(token_queries(q), keys0[(block - 1) * NR : (block + 2) * NR, :]),)

        def weights(block, s0):
            if s0 is None:
                return None, None
            m = jnp.max(s0, axis=1, keepdims=True)
            return m, jnp.exp2((s0 - m) * SCALE2).astype(BF16)

        def products(block, m, p0):
            if m is None:
                return
            at = slice((block - 1) * NR, block * NR)
            x0[head, at, :] = jnp.dot(p0, values0[(block - 1) * NR : (block + 2) * NR, :], preferred_element_type=F32)
            m0[head, at, :] = jnp.broadcast_to(m, (NR, LANES))

        run_stages((scores, weights, products), range(blocks))
        sums = fold_pairs(v_ref[head], k_ref[head])
        for level, out in enumerate((vk1, vk2, vk3), 1):
            if level > 1:
                sums = halve(scratch, sums)
            out[head] = pooled_vk(sums, 2**level)
        return 0

    lax.fori_loop(0, heads, one_head, 0)


def attend_kernel(
    head, q_ref, k_ref, v_ref, x0_in, m0_in, lhs12, lhs3t, vk1, vk2, vk3, first_in, second_in, tops, place,
    att, keys0, values0, halo_vk, scratch,
):
    own, rows = (vk1, vk2, vk3), q_ref.shape[1]
    blocks = rows // HALF
    even = lax.rem(place[0], 2) == 0
    for low in (True, False):

        def halo(index):
            at = slice(index * FAR, (index + 1) * FAR)
            sources = (second_in, first_in) if low else (first_in, second_in)
            return jnp.where(even, sources[0][head, at, :], sources[1][head, at, :])

        k, v = halo(0), halo(1)
        sums = fold_pairs(v, k)
        for level in range(1, LEVELS + 1):
            if level > 1:
                sums = halve(scratch, jnp.concatenate([beyond, sums] if low else [sums, beyond], axis=0))
            far = halo(level + 1)
            base = (2 * level - 2 + (not low)) * NR
            near_at, far_at = (base + FAR, base) if low else (base, base + FAR)
            halo_vk[near_at : near_at + HALF, :] = pooled_vk(sums, 2**level)
            halo_vk[far_at : far_at + FAR, :] = far
            beyond = far.astype(F32) * jnp.where(low_lanes(1), 2.0**level, 2.0 ** (level / 2))
        put_pairs(keys0, values0, 0 if low else 5, k, v)
        for index in range(2):
            start = index * HALF if low else rows - (2 - index) * HALF
            at = slice(start, start + HALF)
            put_pairs(keys0, values0, index + (1 if low else 3), k_ref[head, at, :], v_ref[head, at, :])

    def kept(level, half):
        mine = own[level - 1]
        count, at = mine.shape[1], (half // 2) * NR - NR
        spans = [(at, HALF), (at + 2 * NR, NR)] if half % 2 == 0 else [(at, NR), (at + 2 * NR + HALF, HALF)]
        pieces = []
        for start, size in spans:
            if 0 <= start < count:
                pieces.append(mine[head, start : start + size, :])
            else:
                start += (2 * level - 1) * NR - (count if start > 0 else 0)
                pieces.append(halo_vk[start : start + size, :])
        return jnp.concatenate(pieces, axis=0)

    def side_by_side(upper, lower):
        left = jnp.concatenate([upper, jnp.zeros((upper.shape[0], LANES), BF16)], axis=1)
        right = jnp.concatenate([jnp.zeros((lower.shape[0], LANES), BF16), lower], axis=1)
        return jnp.concatenate([left, right], axis=0)

    top = tops[head]
    positions = top.shape[0]
    lane = lax.broadcasted_iota(jnp.int32, (HALF, LANES), 1)
    distance = lane - HEAD_DIM - place[0]
    distance = jnp.where(distance < 0, distance + positions, distance)
    keep = (lane < HEAD_DIM) | ((distance >= 2) & (distance <= positions - 2))
    lo = low_lanes(HALF)

    def edge_window(block):
        return slice(0, 3 * NR) if block == 0 else slice(3 * NR, 6 * NR)

    def scores(block):
        at = slice(block * HALF, (block + 1) * HALF)
        zero = jnp.zeros((HALF, LANES), BF16)
        left12, left3t = (
            jnp.concatenate([jnp.where(lo, zero, x), jnp.where(lo, zero, swap16(x))], axis=1)
            for x in (lhs12[head, at, :], lhs3t[head, at, :])
        )
        s12 = scores_of(left12, side_by_side(kept(1, block), kept(2, block // 2)))
        s3t = scores_of(left3t, side_by_side(kept(3, block // 4), top))
        s0 = None
        if block in (0, blocks - 1):
            s0 = scores_of(token_queries(q_ref[head, at, :]), keys0[edge_window(block), :])
        return s0, s12, s3t

    def weights(block, s0, s12, s3t):
        masked = jnp.where(keep, s3t[:, LANES:], -jnp.inf)
        su = jnp.concatenate([s12, s3t[:, :LANES], masked], axis=1)
        mu = jnp.max(su, axis=1, keepdims=True)
        pu = jnp.exp2((su - mu) * SCALE2).astype(BF16)
        mu = jnp.concatenate([mu, mu], axis=0)
        if s0 is None:
            m0 = m0_in[head, (block - 1) * NR : block * NR, :]
            m = jnp.maximum(m0, mu)
            return None, jnp.exp2((m0 - m) * SCALE2), pu, jnp.exp2((mu - m) * SCALE2)
        m = jnp.maximum(jnp.max(s0, axis=1, keepdims=True), mu)
        return jnp.exp2((s0 - m) * SCALE2).astype(BF16), None, pu, jnp.exp2((mu - m) * SCALE2)

    def products(block, p0, share0, pu, share):
        values = ones_high(jnp.concatenate([kept(1, block), kept(2, block // 2), kept(3, block // 4), top], axis=0))
        xu = jnp.dot(pu, values, preferred_element_type=F32)
        if p0 is None:
            x = x0_in[head, (block - 1) * NR : block * NR, :] * share0
        else:
            x = jnp.dot(p0, values0[edge_window(block), :], preferred_element_type=F32)
        return x, xu, share

    def finish(block, x, xu, share):
        x = x + jnp.concatenate([xu, xu], axis=0) * share
        x = x / swap(x)
        out = jnp.where(lo, x[:HALF], swap(x[HALF:]))
        att[0, block * HALF : (block + 1) * HALF, :] = out.astype(BF16)

    run_stages((scores, weights, products, finish), range(blocks))


def pair_weights(source, head, group):
    piece = source[head * HEAD_DIM : (head + 1) * HEAD_DIM, group * HEAD_DIM : (group + 1) * HEAD_DIM]
    zero = jnp.zeros_like(piece)
    return jnp.concatenate(
        [jnp.concatenate([piece, zero], axis=1), jnp.concatenate([zero, piece], axis=1)], axis=0
    )


def project_kernel(terms, *refs):
    count = len(terms)
    att, w, rest = refs[:count], refs[count : count + 2], refs[count + 2 :]
    earlier, outs = (rest[:2], rest[2:]) if len(rest) > 2 else (None, rest)
    heads = outs[0].shape[0]
    rows = jnp.concatenate([ref[...] for ref in att], axis=1)
    for core, out in enumerate(outs):
        for group in range(heads):
            columns = [pair_weights(w[source][...], head, core * heads + group) for source, head in terms]
            total = jnp.dot(rows, jnp.concatenate(columns, axis=0), preferred_element_type=F32)
            if earlier:
                total = total + earlier[core][group]
            out[group] = total.astype(out.dtype)


def add_kernel(mine, other, out, total, written):
    copies = []
    for head in range(total.shape[0]):
        total[head] = (mine[head] + other[head].astype(F32)).astype(BF16)
        copies.append(pltpu.make_async_copy(total.at[head], out.at[head], written.at[head]))
        copies[-1].start()
    for copy in copies:
        copy.wait()


def ring(count, step):
    return [(i, (i + step) % count) for i in range(count)]


def exchange(x, axis, bit):
    return lax.ppermute(x, axis, [(i, i ^ bit) for i in range(lax.axis_size(axis))])


def on_device(queries, keys, values, w_out):
    q, k, v = (jnp.transpose(x, (1, 0, 2)) for x in (queries, keys, values))
    heads, rows, _ = q.shape
    groups, count = lax.axis_size("head"), lax.axis_size("seq")
    params = pltpu.CompilerParams(vmem_limit_bytes=VMEM)
    vmem = pl.BlockSpec(memory_space=pltpu.VMEM)

    def shape(size, dtype=BF16):
        return jax.ShapeDtypeStruct((heads, size, LANES), dtype)

    place = lax.axis_index("seq").astype(jnp.int32).reshape(1)
    smem = pl.BlockSpec(memory_space=pltpu.SMEM)
    top, first_out, second_out = pl.pallas_call(
        prepare_kernel,
        in_specs=[pl.BlockSpec(memory_space=pltpu.HBM)] * 2 + [smem],
        out_specs=[vmem] * 3,
        out_shape=[jax.ShapeDtypeStruct((count, heads, LANES), BF16)] + [shape(HALO_ROWS)] * 2,
        scratch_shapes=[pltpu.VMEM((heads, rows, LANES), BF16)] * 2
        + [pltpu.VMEM((heads, rows, LANES), F32), pltpu.SemaphoreType.DMA((heads, 2))],
        compiler_params=pltpu.CompilerParams(vmem_limit_bytes=60 * 1024 * 1024),
        name="prepare",
    )(k, v, place)
    first_in = exchange(first_out, "seq", 1)
    second_in = lax.ppermute(second_out, "seq", [(i, (i - 1 if i % 2 == 0 else i + 1) % count) for i in range(count)])
    tops = lax.all_to_all(top, "seq", split_axis=0, concat_axis=0, tiled=True).transpose(1, 0, 2)
    top, w_out = lax.optimization_barrier((top, w_out))
    width = w_out.shape[1] // groups
    me = jnp.full((1, groups), lax.axis_index("head"), jnp.int32)
    w_own, w_far = pl.pallas_call(
        cut_kernel,
        in_specs=[vmem, pl.BlockSpec(memory_space=pltpu.SMEM)],
        out_shape=[jax.ShapeDtypeStruct((w_out.shape[0], 2 * width), BF16)] * 2,
        compiler_params=params,
        name="cut",
    )(w_out, me)
    w_far = exchange(w_far, "head", 2)

    tops, first_in, q = lax.optimization_barrier((tops, first_in, q))
    pooled = [rows >> level for level in range(LEVELS)]
    inner = pl.pallas_call(
        inner_kernel,
        in_specs=[vmem] * 3,
        out_specs=[vmem] * 7,
        out_shape=[shape(2 * rows - 2 * NR, F32)] * 2 + [shape(rows)] * 2 + [shape(size) for size in pooled],
        scratch_shapes=[pltpu.VMEM((2 * rows, LANES), BF16)] * 2 + [pltpu.VMEM((rows, LANES), F32)],
        compiler_params=params,
        cost_estimate=pl.CostEstimate(flops=4_000_000_000, bytes_accessed=8_000_000, transcendentals=1_000_000),
        name="inner",
    )(q, k, v)
    parts = {}
    for head in range(heads):
        att = pl.pallas_call(
            functools.partial(attend_kernel, head),
            in_specs=[vmem] * 13 + [smem],
            out_shape=jax.ShapeDtypeStruct((1, rows, LANES), BF16),
            scratch_shapes=[pltpu.VMEM((6 * NR, LANES), BF16)] * 3 + [pltpu.VMEM((NR, LANES), F32)],
            compiler_params=params,
            name=f"attend{head}",
        )(q, k, v, *inner, first_in, second_in, tops, place)[0]
        parts[0, head], parts[1, head] = att, exchange(att, "head", 2)
    late = [(1, LAST)]
    early = [term for term in parts if term not in late]
    shares = []
    for terms, types in ((early, (F32, F32)), (late, (F32, BF16))):
        shares = pl.pallas_call(
            functools.partial(project_kernel, terms),
            in_specs=[vmem] * (len(terms) + 2 + len(shares)),
            out_specs=[vmem] * 2,
            out_shape=[shape(rows, dtype) for dtype in types],
            compiler_params=params,
            name="project",
        )(*[parts[term] for term in terms], w_own, w_far, *shares)
    out = pl.pallas_call(
        add_kernel,
        in_specs=[vmem] * 2,
        out_specs=pl.BlockSpec(memory_space=pltpu.HBM),
        scratch_shapes=[pltpu.VMEM((heads, rows, LANES), BF16), pltpu.SemaphoreType.DMA((heads,))],
        out_shape=shape(rows),
        compiler_params=params,
        name="add",
    )(shares[0], exchange(shares[1], "head", 1))
    return jnp.transpose(out, (1, 0, 2))


def solution(mesh):
    return jax.shard_map(
        on_device,
        mesh=mesh,
        in_specs=(
            P("seq", "head", None),
            P("seq", "head", None),
            P("seq", "head", None),
            P("head", None),
        ),
        out_specs=P("seq", "head", None),
        check_vma=False,
    )
```

```python
import functools
import math

import jax
import jax.numpy as jnp
from jax import lax
from jax.experimental import pallas as pl
from jax.experimental.pallas import tpu as pltpu
from jax.sharding import PartitionSpec as P

HEAD_DIM = 64
NR = 128
HALF = NR // 2
LANES = 2 * HEAD_DIM
LEVELS = 3
POOL = 1024
BF16 = jnp.bfloat16
F32 = jnp.float32
SCALE2 = HEAD_DIM ** (-0.5) * math.log2(math.e)
FAR = HALF
VMEM = 16 * 1024 * 1024
LAST = 2
HALO_ROWS = 2 * HALF + LEVELS * FAR


def low_lanes(rows):
    return lax.broadcasted_iota(jnp.int32, (rows, LANES), 1) < HEAD_DIM


def swap(x):
    return pltpu.roll(x, HEAD_DIM, 1)


def swap16(x):
    return pltpu.roll(x, HEAD_DIM, 1)


def fold_pairs(lo, hi):
    lo, hi = lo.astype(F32), hi.astype(F32)
    return jnp.where(low_lanes(lo.shape[0]), lo + swap(lo), hi + swap(hi))


def halve(scratch, x):
    rows = x.shape[0]
    scratch[pl.ds(0, rows), :] = x
    return scratch[pl.ds(0, rows // 2, 2), :] + scratch[pl.ds(1, rows // 2, 2), :]


def pooled_vk(sums, factor):
    scale = jnp.where(low_lanes(1), 1.0 / factor, factor ** (-0.5))
    return (sums * scale).astype(BF16)


def ones_high(v):
    return jnp.where(low_lanes(v.shape[0]), v, jnp.ones_like(v))


def put_pairs(keys, values, block, k, v):
    at = block * NR
    keys[at : at + HALF, :] = k
    keys[at + HALF : at + NR, :] = swap16(k)
    values[at : at + HALF, :] = ones_high(v)
    values[at + HALF : at + NR, :] = ones_high(swap16(v))


def scores_of(lhs, keys):
    return lax.dot_general(lhs, keys, (((1,), (1,)), ((), ())), preferred_element_type=F32)


def group_matrix(rows, shift):
    group = [lax.broadcasted_iota(jnp.int32, (rows, rows), axis) >> shift for axis in range(2)]
    return jnp.where(group[0] == group[1], 1.0, 0.0).astype(BF16)


def prepare_kernel(k_hbm, v_hbm, place, top, first_out, second_out, k, v, scratch, read):
    heads, rows = k.shape[0], k.shape[1]
    even = lax.rem(place[0], 2) == 0
    loads = [
        [
            pltpu.make_async_copy(source.at[head], into.at[head], read.at[head, index])
            for index, (source, into) in enumerate(((k_hbm, k), (v_hbm, v)))
        ]
        for head in range(heads)
    ]
    for pair in loads:
        for copy in pair:
            copy.start()
    for head in range(heads):
        for copy in loads[head]:
            copy.wait()
        lows, highs = [], []
        for source in (k, v):
            lows.append(source[head, 0:HALF, :])
            highs.append(source[head, rows - HALF : rows, :])
        sums = fold_pairs(v[head], k[head])
        for level in range(1, LEVELS + 1):
            if level > 1:
                sums = halve(scratch.at[head], sums)
            vk = pooled_vk(sums, 2**level)
            lows.append(vk[HALF : HALF + FAR])
            highs.append(vk[vk.shape[0] - HALF - FAR : vk.shape[0] - HALF])
        for index, (low, high) in enumerate(zip(lows, highs)):
            at = slice(index * FAR, (index + 1) * FAR)
            first_out[head, at, :] = jnp.where(even, high, low)
            second_out[head, at, :] = jnp.where(even, low, high)
        top[:, head, :] = jnp.broadcast_to(pooled_vk(jnp.sum(sums, axis=0, keepdims=True), POOL), (top.shape[0], LANES))


def cut_kernel(w_ref, me, *outs):
    half, width = outs[0].shape[1], w_ref.shape[1] // me.shape[1]
    for index in range(me.shape[1]):

        @pl.when(me[0, 0] == index)
        def _(index=index):
            for slot, out in enumerate(outs):
                for core in range(2):
                    at = (index ^ (2 * slot + core)) * width
                    out[:, core * width : (core + 1) * width] = w_ref[:, at : at + width]


def run_stages(stages, blocks):
    held = [{} for _ in stages]
    for step in range(len(blocks) + 2 * len(stages)):
        for index, stage in enumerate(stages):
            at = step - 2 * index
            if 0 <= at < len(blocks):
                given = held[index - 1].pop(at) if index else ()
                held[index][at] = stage(blocks[at], *given)


def token_queries(q):
    lo, zero = low_lanes(q.shape[0]), jnp.zeros_like(q)
    return jnp.concatenate([jnp.where(lo, q, zero), jnp.where(lo, swap16(q), zero)], axis=0)


def inner_kernel(q_ref, k_ref, v_ref, x0, m0, lhs12, lhs3t, vk1, vk2, vk3, keys0, values0, scratch):
    heads, rows = q_ref.shape[0], q_ref.shape[1]
    blocks = rows // HALF
    lo = low_lanes(HALF)
    pairs, fours = group_matrix(HALF, 1), group_matrix(HALF, 2)

    def one_head(head, _):
        for block in range(blocks):
            at = slice(block * HALF, (block + 1) * HALF)
            put_pairs(keys0, values0, block, k_ref[head, at, :], v_ref[head, at, :])
        wide = jnp.concatenate([q_ref[head, block * HALF : (block + 1) * HALF, :] for block in range(blocks)], axis=1)
        wide2 = jnp.dot(pairs, wide, preferred_element_type=F32)
        wide3 = jnp.dot(fours, wide, preferred_element_type=F32)
        q_top = jnp.sum(q_ref[head].astype(F32), axis=0, keepdims=True)
        q_top = (q_top + swap(q_top)) * POOL ** (-0.5)

        def queries(block):
            at, lanes = slice(block * HALF, (block + 1) * HALF), slice(block * LANES, (block + 1) * LANES)
            q1, q2, q3 = (
                (sums + swap(sums)) * factor ** (-0.5)
                for sums, factor in ((q_ref[head, at, :].astype(F32), 2), (wide2[:, lanes], 4), (wide3[:, lanes], 8))
            )
            lhs12[head, at, :] = jnp.where(lo, q2, q1).astype(BF16)
            lhs3t[head, at, :] = jnp.where(lo, q_top, q3).astype(BF16)

        def scores(block):
            queries(block)
            if block in (0, blocks - 1):
                return (None,)
            q = q_ref[head, block * HALF : (block + 1) * HALF, :]
            return (scores_of(token_queries(q), keys0[(block - 1) * NR : (block + 2) * NR, :]),)

        def weights(block, s0):
            if s0 is None:
                return None, None
            m = jnp.max(s0, axis=1, keepdims=True)
            return m, jnp.exp2((s0 - m) * SCALE2).astype(BF16)

        def products(block, m, p0):
            if m is None:
                return
            at = slice((block - 1) * NR, block * NR)
            x0[head, at, :] = jnp.dot(p0, values0[(block - 1) * NR : (block + 2) * NR, :], preferred_element_type=F32)
            m0[head, at, :] = jnp.broadcast_to(m, (NR, LANES))

        run_stages((scores, weights, products), range(blocks))
        sums = fold_pairs(v_ref[head], k_ref[head])
        for level, out in enumerate((vk1, vk2, vk3), 1):
            if level > 1:
                sums = halve(scratch, sums)
            out[head] = pooled_vk(sums, 2**level)
        return 0

    lax.fori_loop(0, heads, one_head, 0)


def attend_kernel(
    head, q_ref, k_ref, v_ref, x0_in, m0_in, lhs12, lhs3t, vk1, vk2, vk3, first_in, second_in, tops, place,
    att, keys0, values0, halo_vk, scratch,
):
    own, rows = (vk1, vk2, vk3), q_ref.shape[1]
    blocks = rows // HALF
    even = lax.rem(place[0], 2) == 0
    for low in (True, False):

        def halo(index):
            at = slice(index * FAR, (index + 1) * FAR)
            sources = (second_in, first_in) if low else (first_in, second_in)
            return jnp.where(even, sources[0][head, at, :], sources[1][head, at, :])

        k, v = halo(0), halo(1)
        sums = fold_pairs(v, k)
        for level in range(1, LEVELS + 1):
            if level > 1:
                sums = halve(scratch, jnp.concatenate([beyond, sums] if low else [sums, beyond], axis=0))
            far = halo(level + 1)
            base = (2 * level - 2 + (not low)) * NR
            near_at, far_at = (base + FAR, base) if low else (base, base + FAR)
            halo_vk[near_at : near_at + HALF, :] = pooled_vk(sums, 2**level)
            halo_vk[far_at : far_at + FAR, :] = far
            beyond = far.astype(F32) * jnp.where(low_lanes(1), 2.0**level, 2.0 ** (level / 2))
        put_pairs(keys0, values0, 0 if low else 5, k, v)
        for index in range(2):
            start = index * HALF if low else rows - (2 - index) * HALF
            at = slice(start, start + HALF)
            put_pairs(keys0, values0, index + (1 if low else 3), k_ref[head, at, :], v_ref[head, at, :])

    def kept(level, half):
        mine = own[level - 1]
        count, at = mine.shape[1], (half // 2) * NR - NR
        spans = [(at, HALF), (at + 2 * NR, NR)] if half % 2 == 0 else [(at, NR), (at + 2 * NR + HALF, HALF)]
        pieces = []
        for start, size in spans:
            if 0 <= start < count:
                pieces.append(mine[head, start : start + size, :])
            else:
                start += (2 * level - 1) * NR - (count if start > 0 else 0)
                pieces.append(halo_vk[start : start + size, :])
        return jnp.concatenate(pieces, axis=0)

    def side_by_side(upper, lower):
        left = jnp.concatenate([upper, jnp.zeros((upper.shape[0], LANES), BF16)], axis=1)
        right = jnp.concatenate([jnp.zeros((lower.shape[0], LANES), BF16), lower], axis=1)
        return jnp.concatenate([left, right], axis=0)

    top = tops[head]
    positions = top.shape[0]
    lane = lax.broadcasted_iota(jnp.int32, (HALF, LANES), 1)
    distance = lane - HEAD_DIM - place[0]
    distance = jnp.where(distance < 0, distance + positions, distance)
    keep = (lane < HEAD_DIM) | ((distance >= 2) & (distance <= positions - 2))
    lo = low_lanes(HALF)

    def edge_window(block):
        return slice(0, 3 * NR) if block == 0 else slice(3 * NR, 6 * NR)

    def apart(x):
        low, zero = low_lanes(x.shape[0]), jnp.zeros_like(x)
        return jnp.concatenate([jnp.where(low, zero, x), jnp.where(low, zero, swap16(x))], axis=1)

    shared, shared_x, waiting, unfinished = {}, {}, [], []

    def scores(block):
        at = slice(block * HALF, (block + 1) * HALF)
        s12 = scores_of(apart(lhs12[head, at, :]), side_by_side(kept(1, block), kept(2, block // 2)))
        if block % 4 == 0:
            four = slice(block * HALF, (block + 4) * HALF)
            shared[block // 4] = scores_of(apart(lhs3t[head, four, :]), side_by_side(kept(3, block // 4), top))
        s3t = shared[block // 4][(block % 4) * HALF : (block % 4 + 1) * HALF]
        s0 = None
        if block in (0, blocks - 1):
            s0 = scores_of(token_queries(q_ref[head, at, :]), keys0[edge_window(block), :])
        return s0, s12, s3t

    def weights(block, s0, s12, s3t):
        masked = jnp.where(keep, s3t[:, LANES:], -jnp.inf)
        su = jnp.concatenate([s12, s3t[:, :LANES], masked], axis=1)
        mu = jnp.max(su, axis=1, keepdims=True)
        pu = jnp.exp2((su - mu) * SCALE2).astype(BF16)
        mu = jnp.concatenate([mu, mu], axis=0)
        if s0 is None:
            m0 = m0_in[head, (block - 1) * NR : block * NR, :]
            m = jnp.maximum(m0, mu)
            return None, jnp.exp2((m0 - m) * SCALE2), pu, jnp.exp2((mu - m) * SCALE2)
        m = jnp.maximum(jnp.max(s0, axis=1, keepdims=True), mu)
        return jnp.exp2((s0 - m) * SCALE2).astype(BF16), None, pu, jnp.exp2((mu - m) * SCALE2)

    def products(block, p0, share0, pu, share):
        values = ones_high(jnp.concatenate([kept(1, block), kept(2, block // 2)], axis=0))
        split = values.shape[0]
        xu = jnp.dot(pu[:, :split], values, preferred_element_type=F32)
        waiting.append(pu[:, split:])
        if block % 4 == 3:
            values = ones_high(jnp.concatenate([kept(3, block // 4), top], axis=0))
            shared_x[block // 4] = jnp.dot(jnp.concatenate(waiting, axis=0), values, preferred_element_type=F32)
            waiting.clear()
        if p0 is None:
            x = x0_in[head, (block - 1) * NR : block * NR, :] * share0
        else:
            x = jnp.dot(p0, values0[edge_window(block), :], preferred_element_type=F32)
        return x, xu, share

    def finish(block, x, xu, share):
        unfinished.append((block, x, xu, share))
        if block % 4 == 3:
            for item in unfinished:
                finish_one(*item)
            unfinished.clear()

    def finish_one(block, x, xu, share):
        xu = xu + shared_x[block // 4][(block % 4) * HALF : (block % 4 + 1) * HALF]
        x = x + jnp.concatenate([xu, xu], axis=0) * share
        x = x / swap(x)
        out = jnp.where(lo, x[:HALF], swap(x[HALF:]))
        att[0, block * HALF : (block + 1) * HALF, :] = out.astype(BF16)

    run_stages((scores, weights, products, finish), range(blocks))


def pair_weights(source, head, group):
    piece = source[head * HEAD_DIM : (head + 1) * HEAD_DIM, group * HEAD_DIM : (group + 1) * HEAD_DIM]
    zero = jnp.zeros_like(piece)
    return jnp.concatenate(
        [jnp.concatenate([piece, zero], axis=1), jnp.concatenate([zero, piece], axis=1)], axis=0
    )


def project_kernel(terms, *refs):
    count = len(terms)
    att, w, rest = refs[:count], refs[count : count + 2], refs[count + 2 :]
    earlier, outs = (rest[:2], rest[2:]) if len(rest) > 2 else (None, rest)
    heads = outs[0].shape[0]
    rows = jnp.concatenate([ref[...] for ref in att], axis=1)
    for core, out in enumerate(outs):
        for group in range(heads):
            columns = [pair_weights(w[source][...], head, core * heads + group) for source, head in terms]
            total = jnp.dot(rows, jnp.concatenate(columns, axis=0), preferred_element_type=F32)
            if earlier:
                total = total + earlier[core][group]
            out[group] = total.astype(out.dtype)


def add_kernel(mine, other, out, total, written):
    copies = []
    for head in range(total.shape[0]):
        total[head] = (mine[head] + other[head].astype(F32)).astype(BF16)
        copies.append(pltpu.make_async_copy(total.at[head], out.at[head], written.at[head]))
        copies[-1].start()
    for copy in copies:
        copy.wait()


def ring(count, step):
    return [(i, (i + step) % count) for i in range(count)]


def exchange(x, axis, bit):
    return lax.ppermute(x, axis, [(i, i ^ bit) for i in range(lax.axis_size(axis))])


def on_device(queries, keys, values, w_out):
    q, k, v = (jnp.transpose(x, (1, 0, 2)) for x in (queries, keys, values))
    heads, rows, _ = q.shape
    groups, count = lax.axis_size("head"), lax.axis_size("seq")
    params = pltpu.CompilerParams(vmem_limit_bytes=VMEM)
    vmem = pl.BlockSpec(memory_space=pltpu.VMEM)

    def shape(size, dtype=BF16):
        return jax.ShapeDtypeStruct((heads, size, LANES), dtype)

    place = lax.axis_index("seq").astype(jnp.int32).reshape(1)
    smem = pl.BlockSpec(memory_space=pltpu.SMEM)
    top, first_out, second_out = pl.pallas_call(
        prepare_kernel,
        in_specs=[pl.BlockSpec(memory_space=pltpu.HBM)] * 2 + [smem],
        out_specs=[vmem] * 3,
        out_shape=[jax.ShapeDtypeStruct((count, heads, LANES), BF16)] + [shape(HALO_ROWS)] * 2,
        scratch_shapes=[pltpu.VMEM((heads, rows, LANES), BF16)] * 2
        + [pltpu.VMEM((heads, rows, LANES), F32), pltpu.SemaphoreType.DMA((heads, 2))],
        compiler_params=pltpu.CompilerParams(vmem_limit_bytes=60 * 1024 * 1024),
        name="prepare",
    )(k, v, place)
    first_in = exchange(first_out, "seq", 1)
    second_in = lax.ppermute(second_out, "seq", [(i, (i - 1 if i % 2 == 0 else i + 1) % count) for i in range(count)])
    tops = lax.all_to_all(top, "seq", split_axis=0, concat_axis=0, tiled=True).transpose(1, 0, 2)
    top, w_out = lax.optimization_barrier((top, w_out))
    width = w_out.shape[1] // groups
    me = jnp.full((1, groups), lax.axis_index("head"), jnp.int32)
    w_own, w_far = pl.pallas_call(
        cut_kernel,
        in_specs=[vmem, pl.BlockSpec(memory_space=pltpu.SMEM)],
        out_shape=[jax.ShapeDtypeStruct((w_out.shape[0], 2 * width), BF16)] * 2,
        compiler_params=params,
        name="cut",
    )(w_out, me)
    w_far = exchange(w_far, "head", 2)

    tops, first_in, q = lax.optimization_barrier((tops, first_in, q))
    pooled = [rows >> level for level in range(LEVELS)]
    inner = pl.pallas_call(
        inner_kernel,
        in_specs=[vmem] * 3,
        out_specs=[vmem] * 7,
        out_shape=[shape(2 * rows - 2 * NR, F32)] * 2 + [shape(rows)] * 2 + [shape(size) for size in pooled],
        scratch_shapes=[pltpu.VMEM((2 * rows, LANES), BF16)] * 2 + [pltpu.VMEM((rows, LANES), F32)],
        compiler_params=params,
        cost_estimate=pl.CostEstimate(flops=4_000_000_000, bytes_accessed=8_000_000, transcendentals=1_000_000),
        name="inner",
    )(q, k, v)
    parts = {}
    for head in range(heads):
        att = pl.pallas_call(
            functools.partial(attend_kernel, head),
            in_specs=[vmem] * 13 + [smem],
            out_shape=jax.ShapeDtypeStruct((1, rows, LANES), BF16),
            scratch_shapes=[pltpu.VMEM((6 * NR, LANES), BF16)] * 3 + [pltpu.VMEM((NR, LANES), F32)],
            compiler_params=params,
            name=f"attend{head}",
        )(q, k, v, *inner, first_in, second_in, tops, place)[0]
        parts[0, head], parts[1, head] = att, exchange(att, "head", 2)
    late = [(1, LAST)]
    early = [term for term in parts if term not in late]
    shares = []
    for terms, types in ((early, (F32, F32)), (late, (F32, BF16))):
        shares = pl.pallas_call(
            functools.partial(project_kernel, terms),
            in_specs=[vmem] * (len(terms) + 2 + len(shares)),
            out_specs=[vmem] * 2,
            out_shape=[shape(rows, dtype) for dtype in types],
            compiler_params=params,
            name="project",
        )(*[parts[term] for term in terms], w_own, w_far, *shares)
    out = pl.pallas_call(
        add_kernel,
        in_specs=[vmem] * 2,
        out_specs=pl.BlockSpec(memory_space=pltpu.HBM),
        scratch_shapes=[pltpu.VMEM((heads, rows, LANES), BF16), pltpu.SemaphoreType.DMA((heads,))],
        out_shape=shape(rows),
        compiler_params=params,
        name="add",
    )(shares[0], exchange(shares[1], "head", 1))
    return jnp.transpose(out, (1, 0, 2))


def solution(mesh):
    return jax.shard_map(
        on_device,
        mesh=mesh,
        in_specs=(
            P("seq", "head", None),
            P("seq", "head", None),
            P("seq", "head", None),
            P("head", None),
        ),
        out_specs=P("seq", "head", None),
        check_vma=False,
    )
```

```python
import functools
import math

import jax
import jax.numpy as jnp
from jax import lax
from jax.experimental import pallas as pl
from jax.experimental.pallas import tpu as pltpu
from jax.sharding import PartitionSpec as P

HEAD_DIM = 64
NR = 128
HALF = NR // 2
LANES = 2 * HEAD_DIM
LEVELS = 3
POOL = 1024
BF16 = jnp.bfloat16
F32 = jnp.float32
SCALE2 = HEAD_DIM ** (-0.5) * math.log2(math.e)
FAR = HALF
VMEM = 16 * 1024 * 1024
LAST = 2
HALO_ROWS = 2 * HALF + LEVELS * FAR


def low_lanes(rows):
    return lax.broadcasted_iota(jnp.int32, (rows, LANES), 1) < HEAD_DIM


def swap(x):
    return pltpu.roll(x, HEAD_DIM, 1)


def swap16(x):
    return pltpu.roll(x, HEAD_DIM, 1)


def fold_pairs(lo, hi):
    lo, hi = lo.astype(F32), hi.astype(F32)
    return jnp.where(low_lanes(lo.shape[0]), lo + swap(lo), hi + swap(hi))


def halve(scratch, x):
    rows = x.shape[0]
    scratch[pl.ds(0, rows), :] = x
    return scratch[pl.ds(0, rows // 2, 2), :] + scratch[pl.ds(1, rows // 2, 2), :]


def pooled_vk(sums, factor):
    scale = jnp.where(low_lanes(1), 1.0 / factor, factor ** (-0.5))
    return (sums * scale).astype(BF16)


def ones_high(v):
    return jnp.where(low_lanes(v.shape[0]), v, jnp.ones_like(v))


def put_pairs(keys, values, block, k, v):
    at = block * NR
    keys[at : at + HALF, :] = k
    keys[at + HALF : at + NR, :] = swap16(k)
    values[at : at + HALF, :] = ones_high(v)
    values[at + HALF : at + NR, :] = ones_high(swap16(v))


def scores_of(lhs, keys):
    return lax.dot_general(lhs, keys, (((1,), (1,)), ((), ())), preferred_element_type=F32)


def group_matrix(rows, shift):
    group = [lax.broadcasted_iota(jnp.int32, (rows, rows), axis) >> shift for axis in range(2)]
    return jnp.where(group[0] == group[1], 1.0, 0.0).astype(BF16)


def prepare_kernel(k_hbm, v_hbm, place, top, first_out, second_out, k, v, scratch, read):
    heads, rows = k.shape[0], k.shape[1]
    even = lax.rem(place[0], 2) == 0
    loads = [
        [
            pltpu.make_async_copy(source.at[head], into.at[head], read.at[head, index])
            for index, (source, into) in enumerate(((k_hbm, k), (v_hbm, v)))
        ]
        for head in range(heads)
    ]
    for pair in loads:
        for copy in pair:
            copy.start()
    coarse = []
    for head in range(heads):
        for copy in loads[head]:
            copy.wait()
        lows, highs = [], []
        for source in (k, v):
            lows.append(source[head, 0:HALF, :])
            highs.append(source[head, rows - HALF : rows, :])
        sums = fold_pairs(v[head], k[head])
        for level in range(1, LEVELS + 1):
            if level > 1:
                sums = halve(scratch.at[head], sums)
            vk = pooled_vk(sums, 2**level)
            lows.append(vk[HALF : HALF + FAR])
            highs.append(vk[vk.shape[0] - HALF - FAR : vk.shape[0] - HALF])
        for index, (low, high) in enumerate(zip(lows, highs)):
            at = slice(index * FAR, (index + 1) * FAR)
            first_out[head, at, :] = jnp.where(even, high, low)
            second_out[head, at, :] = jnp.where(even, low, high)
        coarse.append(jnp.sum(sums, axis=0, keepdims=True))
    rows = pooled_vk(jnp.concatenate(coarse, axis=0), POOL)
    for position in range(top.shape[0]):
        top[position] = rows


def cut_kernel(w_ref, me, *outs):
    half, width = outs[0].shape[1], w_ref.shape[1] // me.shape[1]
    for index in range(me.shape[1]):

        @pl.when(me[0, 0] == index)
        def _(index=index):
            for slot, out in enumerate(outs):
                for core in range(2):
                    at = (index ^ (2 * slot + core)) * width
                    out[:, core * width : (core + 1) * width] = w_ref[:, at : at + width]


def run_stages(stages, blocks):
    held = [{} for _ in stages]
    for step in range(len(blocks) + 2 * len(stages)):
        for index, stage in enumerate(stages):
            at = step - 2 * index
            if 0 <= at < len(blocks):
                given = held[index - 1].pop(at) if index else ()
                held[index][at] = stage(blocks[at], *given)


def token_queries(q):
    lo, zero = low_lanes(q.shape[0]), jnp.zeros_like(q)
    return jnp.concatenate([jnp.where(lo, q, zero), jnp.where(lo, swap16(q), zero)], axis=0)


def inner_kernel(q_ref, k_ref, v_ref, x0, m0, lhs12, lhs3t, vk1, vk2, vk3, keys0, values0, scratch):
    heads, rows = q_ref.shape[0], q_ref.shape[1]
    blocks = rows // HALF
    lo = low_lanes(HALF)
    pairs, fours = group_matrix(HALF, 1), group_matrix(HALF, 2)

    shared = {}

    def start(task):
        head, block = task
        if block == 0:
            for index in range(blocks):
                at = slice(index * HALF, (index + 1) * HALF)
                put_pairs(keys0.at[head], values0.at[head], index, k_ref[head, at, :], v_ref[head, at, :])
            wide = jnp.concatenate([q_ref[head, i * HALF : (i + 1) * HALF, :] for i in range(blocks)], axis=1)
            wide2 = jnp.dot(pairs, wide, preferred_element_type=F32)
            wide3 = jnp.dot(fours, wide, preferred_element_type=F32)
            q_top = jnp.sum(q_ref[head].astype(F32), axis=0, keepdims=True)
            shared[head] = wide2, wide3, (q_top + swap(q_top)) * POOL ** (-0.5)
        if block == 4:
            sums = fold_pairs(v_ref[head], k_ref[head])
            for level, out in enumerate((vk1, vk2, vk3), 1):
                if level > 1:
                    sums = halve(scratch.at[head], sums)
                out[head] = pooled_vk(sums, 2**level)
        return ()

    def scores(task):
        head, block = task
        at, lanes = slice(block * HALF, (block + 1) * HALF), slice(block * LANES, (block + 1) * LANES)
        wide2, wide3, q_top = shared[head]
        q1, q2, q3 = (
            (sums + swap(sums)) * factor ** (-0.5)
            for sums, factor in ((q_ref[head, at, :].astype(F32), 2), (wide2[:, lanes], 4), (wide3[:, lanes], 8))
        )
        lhs12[head, at, :] = jnp.where(lo, q2, q1).astype(BF16)
        lhs3t[head, at, :] = jnp.where(lo, q_top, q3).astype(BF16)
        if block in (0, blocks - 1):
            return (None,)
        return (scores_of(token_queries(q_ref[head, at, :]), keys0[head, (block - 1) * NR : (block + 2) * NR, :]),)

    def weights(task, s0):
        if s0 is None:
            return None, None
        m = jnp.max(s0, axis=1, keepdims=True)
        return m, jnp.exp2((s0 - m) * SCALE2).astype(BF16)

    def products(task, m, p0):
        head, block = task
        if m is None:
            return
        at, window = slice((block - 1) * NR, block * NR), slice((block - 1) * NR, (block + 2) * NR)
        x0[head, at, :] = jnp.dot(p0, values0[head, window, :], preferred_element_type=F32)
        m0[head, at, :] = jnp.broadcast_to(m, (NR, LANES))

    run_stages((start, scores, weights, products), [(head, block) for head in range(heads) for block in range(blocks)])


def attend_kernel(
    head, q_ref, k_ref, v_ref, x0_in, m0_in, lhs12, lhs3t, vk1, vk2, vk3, first_in, second_in, tops, place,
    att, keys0, values0, halo_vk, scratch,
):
    own, rows = (vk1, vk2, vk3), q_ref.shape[1]
    blocks = rows // HALF
    even = lax.rem(place[0], 2) == 0
    for low in (True, False):

        def halo(index):
            at = slice(index * FAR, (index + 1) * FAR)
            sources = (second_in, first_in) if low else (first_in, second_in)
            return jnp.where(even, sources[0][head, at, :], sources[1][head, at, :])

        k, v = halo(0), halo(1)
        sums = fold_pairs(v, k)
        for level in range(1, LEVELS + 1):
            if level > 1:
                sums = halve(scratch, jnp.concatenate([beyond, sums] if low else [sums, beyond], axis=0))
            far = halo(level + 1)
            base = (2 * level - 2 + (not low)) * NR
            near_at, far_at = (base + FAR, base) if low else (base, base + FAR)
            halo_vk[near_at : near_at + HALF, :] = pooled_vk(sums, 2**level)
            halo_vk[far_at : far_at + FAR, :] = far
            beyond = far.astype(F32) * jnp.where(low_lanes(1), 2.0**level, 2.0 ** (level / 2))
        put_pairs(keys0, values0, 0 if low else 5, k, v)
        for index in range(2):
            start = index * HALF if low else rows - (2 - index) * HALF
            at = slice(start, start + HALF)
            put_pairs(keys0, values0, index + (1 if low else 3), k_ref[head, at, :], v_ref[head, at, :])

    def kept(level, half):
        mine = own[level - 1]
        count, at = mine.shape[1], (half // 2) * NR - NR
        spans = [(at, HALF), (at + 2 * NR, NR)] if half % 2 == 0 else [(at, NR), (at + 2 * NR + HALF, HALF)]
        pieces = []
        for start, size in spans:
            if 0 <= start < count:
                pieces.append(mine[head, start : start + size, :])
            else:
                start += (2 * level - 1) * NR - (count if start > 0 else 0)
                pieces.append(halo_vk[start : start + size, :])
        return jnp.concatenate(pieces, axis=0)

    def side_by_side(upper, lower):
        left = jnp.concatenate([upper, jnp.zeros((upper.shape[0], LANES), BF16)], axis=1)
        right = jnp.concatenate([jnp.zeros((lower.shape[0], LANES), BF16), lower], axis=1)
        return jnp.concatenate([left, right], axis=0)

    top = tops[head]
    positions = top.shape[0]
    lane = lax.broadcasted_iota(jnp.int32, (HALF, LANES), 1)
    distance = lane - HEAD_DIM - place[0]
    distance = jnp.where(distance < 0, distance + positions, distance)
    keep = (lane < HEAD_DIM) | ((distance >= 2) & (distance <= positions - 2))
    lo = low_lanes(HALF)

    def edge_window(block):
        return slice(0, 3 * NR) if block == 0 else slice(3 * NR, 6 * NR)

    def apart(x):
        low, zero = low_lanes(x.shape[0]), jnp.zeros_like(x)
        return jnp.concatenate([jnp.where(low, zero, x), jnp.where(low, zero, swap16(x))], axis=1)

    shared, shared_x, waiting, unfinished = {}, {}, [], []

    def scores(block):
        at = slice(block * HALF, (block + 1) * HALF)
        s12 = scores_of(apart(lhs12[head, at, :]), side_by_side(kept(1, block), kept(2, block // 2)))
        if block % 4 == 0:
            four = slice(block * HALF, (block + 4) * HALF)
            shared[block // 4] = scores_of(apart(lhs3t[head, four, :]), side_by_side(kept(3, block // 4), top))
        s3t = shared[block // 4][(block % 4) * HALF : (block % 4 + 1) * HALF]
        s0 = None
        if block in (0, blocks - 1):
            s0 = scores_of(token_queries(q_ref[head, at, :]), keys0[edge_window(block), :])
        return s0, s12, s3t

    def weights(block, s0, s12, s3t):
        masked = jnp.where(keep, s3t[:, LANES:], -jnp.inf)
        su = jnp.concatenate([s12, s3t[:, :LANES], masked], axis=1)
        mu = jnp.max(su, axis=1, keepdims=True)
        pu = jnp.exp2((su - mu) * SCALE2).astype(BF16)
        mu = jnp.concatenate([mu, mu], axis=0)
        if s0 is None:
            m0 = m0_in[head, (block - 1) * NR : block * NR, :]
            m = jnp.maximum(m0, mu)
            return None, jnp.exp2((m0 - m) * SCALE2), pu, jnp.exp2((mu - m) * SCALE2)
        m = jnp.maximum(jnp.max(s0, axis=1, keepdims=True), mu)
        return jnp.exp2((s0 - m) * SCALE2).astype(BF16), None, pu, jnp.exp2((mu - m) * SCALE2)

    def products(block, p0, share0, pu, share):
        values = ones_high(jnp.concatenate([kept(1, block), kept(2, block // 2)], axis=0))
        split = values.shape[0]
        xu = jnp.dot(pu[:, :split], values, preferred_element_type=F32)
        waiting.append(pu[:, split:])
        if block % 4 == 3:
            values = ones_high(jnp.concatenate([kept(3, block // 4), top], axis=0))
            shared_x[block // 4] = jnp.dot(jnp.concatenate(waiting, axis=0), values, preferred_element_type=F32)
            waiting.clear()
        if p0 is None:
            x = x0_in[head, (block - 1) * NR : block * NR, :] * share0
        else:
            x = jnp.dot(p0, values0[edge_window(block), :], preferred_element_type=F32)
        return x, xu, share

    def finish(block, x, xu, share):
        unfinished.append((block, x, xu, share))
        if block % 4 == 3:
            for item in unfinished:
                finish_one(*item)
            unfinished.clear()

    def finish_one(block, x, xu, share):
        xu = xu + shared_x[block // 4][(block % 4) * HALF : (block % 4 + 1) * HALF]
        x = x + jnp.concatenate([xu, xu], axis=0) * share
        x = x / swap(x)
        out = jnp.where(lo, x[:HALF], swap(x[HALF:]))
        att[0, block * HALF : (block + 1) * HALF, :] = out.astype(BF16)

    run_stages((scores, weights, products, finish), range(blocks))


def pair_weights(source, head, group):
    piece = source[head * HEAD_DIM : (head + 1) * HEAD_DIM, group * HEAD_DIM : (group + 1) * HEAD_DIM]
    zero = jnp.zeros_like(piece)
    return jnp.concatenate(
        [jnp.concatenate([piece, zero], axis=1), jnp.concatenate([zero, piece], axis=1)], axis=0
    )


def project_kernel(terms, *refs):
    count = len(terms)
    att, w, rest = refs[:count], refs[count : count + 2], refs[count + 2 :]
    earlier, outs = (rest[:2], rest[2:]) if len(rest) > 2 else (None, rest)
    heads = outs[0].shape[0]
    rows = jnp.concatenate([ref[...] for ref in att], axis=1)
    for core, out in enumerate(outs):
        for group in range(heads):
            columns = [pair_weights(w[source][...], head, core * heads + group) for source, head in terms]
            total = jnp.dot(rows, jnp.concatenate(columns, axis=0), preferred_element_type=F32)
            if earlier:
                total = total + earlier[core][group]
            out[group] = total.astype(out.dtype)


def add_kernel(mine, other, out, total, written):
    copies = []
    for head in range(total.shape[0]):
        total[head] = (mine[head] + other[head].astype(F32)).astype(BF16)
        copies.append(pltpu.make_async_copy(total.at[head], out.at[head], written.at[head]))
        copies[-1].start()
    for copy in copies:
        copy.wait()


def ring(count, step):
    return [(i, (i + step) % count) for i in range(count)]


def exchange(x, axis, bit):
    return lax.ppermute(x, axis, [(i, i ^ bit) for i in range(lax.axis_size(axis))])


def on_device(queries, keys, values, w_out):
    q, k, v = (jnp.transpose(x, (1, 0, 2)) for x in (queries, keys, values))
    heads, rows, _ = q.shape
    groups, count = lax.axis_size("head"), lax.axis_size("seq")
    params = pltpu.CompilerParams(vmem_limit_bytes=VMEM)
    vmem = pl.BlockSpec(memory_space=pltpu.VMEM)

    def shape(size, dtype=BF16):
        return jax.ShapeDtypeStruct((heads, size, LANES), dtype)

    place = lax.axis_index("seq").astype(jnp.int32).reshape(1)
    smem = pl.BlockSpec(memory_space=pltpu.SMEM)
    top, first_out, second_out = pl.pallas_call(
        prepare_kernel,
        in_specs=[pl.BlockSpec(memory_space=pltpu.HBM)] * 2 + [smem],
        out_specs=[vmem] * 3,
        out_shape=[jax.ShapeDtypeStruct((count, heads, LANES), BF16)] + [shape(HALO_ROWS)] * 2,
        scratch_shapes=[pltpu.VMEM((heads, rows, LANES), BF16)] * 2
        + [pltpu.VMEM((heads, rows, LANES), F32), pltpu.SemaphoreType.DMA((heads, 2))],
        compiler_params=pltpu.CompilerParams(vmem_limit_bytes=60 * 1024 * 1024),
        name="prepare",
    )(k, v, place)
    first_in = exchange(first_out, "seq", 1)
    second_in = lax.ppermute(second_out, "seq", [(i, (i - 1 if i % 2 == 0 else i + 1) % count) for i in range(count)])
    tops = lax.all_to_all(top, "seq", split_axis=0, concat_axis=0, tiled=True).transpose(1, 0, 2)
    top, w_out = lax.optimization_barrier((top, w_out))
    width = w_out.shape[1] // groups
    me = jnp.full((1, groups), lax.axis_index("head"), jnp.int32)
    w_own, w_far = pl.pallas_call(
        cut_kernel,
        in_specs=[vmem, pl.BlockSpec(memory_space=pltpu.SMEM)],
        out_shape=[jax.ShapeDtypeStruct((w_out.shape[0], 2 * width), BF16)] * 2,
        compiler_params=params,
        name="cut",
    )(w_out, me)
    w_far = exchange(w_far, "head", 2)

    tops, first_in, q = lax.optimization_barrier((tops, first_in, q))
    pooled = [rows >> level for level in range(LEVELS)]
    inner = pl.pallas_call(
        inner_kernel,
        in_specs=[vmem] * 3,
        out_specs=[vmem] * 7,
        out_shape=[shape(2 * rows - 2 * NR, F32)] * 2 + [shape(rows)] * 2 + [shape(size) for size in pooled],
        scratch_shapes=[pltpu.VMEM((heads, 2 * rows, LANES), BF16)] * 2 + [pltpu.VMEM((heads, rows, LANES), F32)],
        compiler_params=params,
        cost_estimate=pl.CostEstimate(flops=4_000_000_000, bytes_accessed=8_000_000, transcendentals=1_000_000),
        name="inner",
    )(q, k, v)
    parts = {}
    for head in range(heads):
        att = pl.pallas_call(
            functools.partial(attend_kernel, head),
            in_specs=[vmem] * 13 + [smem],
            out_shape=jax.ShapeDtypeStruct((1, rows, LANES), BF16),
            scratch_shapes=[pltpu.VMEM((6 * NR, LANES), BF16)] * 3 + [pltpu.VMEM((NR, LANES), F32)],
            compiler_params=params,
            name=f"attend{head}",
        )(q, k, v, *inner, first_in, second_in, tops, place)[0]
        parts[0, head], parts[1, head] = att, exchange(att, "head", 2)
    late = [(1, LAST)]
    early = [term for term in parts if term not in late]
    shares = []
    for terms, types in ((early, (F32, F32)), (late, (F32, BF16))):
        shares = pl.pallas_call(
            functools.partial(project_kernel, terms),
            in_specs=[vmem] * (len(terms) + 2 + len(shares)),
            out_specs=[vmem] * 2,
            out_shape=[shape(rows, dtype) for dtype in types],
            compiler_params=params,
            name="project",
        )(*[parts[term] for term in terms], w_own, w_far, *shares)
    out = pl.pallas_call(
        add_kernel,
        in_specs=[vmem] * 2,
        out_specs=pl.BlockSpec(memory_space=pltpu.HBM),
        scratch_shapes=[pltpu.VMEM((heads, rows, LANES), BF16), pltpu.SemaphoreType.DMA((heads,))],
        out_shape=shape(rows),
        compiler_params=params,
        name="add",
    )(shares[0], exchange(shares[1], "head", 1))
    return jnp.transpose(out, (1, 0, 2))


def solution(mesh):
    return jax.shard_map(
        on_device,
        mesh=mesh,
        in_specs=(
            P("seq", "head", None),
            P("seq", "head", None),
            P("seq", "head", None),
            P("head", None),
        ),
        out_specs=P("seq", "head", None),
        check_vma=False,
    )
```

```python
import functools
import math

import jax
import jax.numpy as jnp
from jax import lax
from jax.experimental import pallas as pl
from jax.experimental.pallas import tpu as pltpu
from jax.sharding import PartitionSpec as P

HEAD_DIM = 64
NR = 128
HALF = NR // 2
LANES = 2 * HEAD_DIM
LEVELS = 3
POOL = 1024
BF16 = jnp.bfloat16
F32 = jnp.float32
SCALE2 = HEAD_DIM ** (-0.5) * math.log2(math.e)
FAR = HALF
VMEM = 16 * 1024 * 1024
LAST = 2
HALO_ROWS = 2 * HALF + LEVELS * FAR


def low_lanes(rows):
    return lax.broadcasted_iota(jnp.int32, (rows, LANES), 1) < HEAD_DIM


def swap(x):
    return pltpu.roll(x, HEAD_DIM, 1)


def swap16(x):
    return pltpu.roll(x, HEAD_DIM, 1)


def fold_pairs(lo, hi):
    lo, hi = lo.astype(F32), hi.astype(F32)
    return jnp.where(low_lanes(lo.shape[0]), lo + swap(lo), hi + swap(hi))


def halve(scratch, x):
    rows = x.shape[0]
    scratch[pl.ds(0, rows), :] = x
    return scratch[pl.ds(0, rows // 2, 2), :] + scratch[pl.ds(1, rows // 2, 2), :]


def pooled_vk(sums, factor):
    scale = jnp.where(low_lanes(1), 1.0 / factor, factor ** (-0.5))
    return (sums * scale).astype(BF16)


def ones_high(v):
    return jnp.where(low_lanes(v.shape[0]), v, jnp.ones_like(v))


def put_pairs(keys, values, block, k, v):
    at = block * NR
    keys[at : at + HALF, :] = k
    keys[at + HALF : at + NR, :] = swap16(k)
    values[at : at + HALF, :] = ones_high(v)
    values[at + HALF : at + NR, :] = ones_high(swap16(v))


def scores_of(lhs, keys):
    return lax.dot_general(lhs, keys, (((1,), (1,)), ((), ())), preferred_element_type=F32)


def group_matrix(rows, shift):
    group = [lax.broadcasted_iota(jnp.int32, (rows, rows), axis) >> shift for axis in range(2)]
    return jnp.where(group[0] == group[1], 1.0, 0.0).astype(BF16)


def prepare_kernel(k_hbm, v_hbm, place, top, first_out, second_out, k, v, scratch, read):
    heads, rows = k.shape[0], k.shape[1]
    even = lax.rem(place[0], 2) == 0
    loads = [
        [
            pltpu.make_async_copy(source.at[head], into.at[head], read.at[head, index])
            for index, (source, into) in enumerate(((k_hbm, k), (v_hbm, v)))
        ]
        for head in range(heads)
    ]
    for pair in loads:
        for copy in pair:
            copy.start()
    coarse = []
    for head in range(heads):
        for copy in loads[head]:
            copy.wait()
        lows, highs = [], []
        for source in (k, v):
            lows.append(source[head, 0:HALF, :])
            highs.append(source[head, rows - HALF : rows, :])
        sums = fold_pairs(v[head], k[head])
        for level in range(1, LEVELS + 1):
            if level > 1:
                sums = halve(scratch.at[head], sums)
            vk = pooled_vk(sums, 2**level)
            lows.append(vk[HALF : HALF + FAR])
            highs.append(vk[vk.shape[0] - HALF - FAR : vk.shape[0] - HALF])
        for index, (low, high) in enumerate(zip(lows, highs)):
            at = slice(index * FAR, (index + 1) * FAR)
            first_out[head, at, :] = jnp.where(even, high, low)
            second_out[head, at, :] = jnp.where(even, low, high)
        coarse.append(jnp.sum(sums, axis=0, keepdims=True))
    rows = pooled_vk(jnp.concatenate(coarse, axis=0), POOL)
    for position in range(top.shape[0]):
        top[position] = rows


def cut_kernel(w_ref, me, *outs):
    half, width = outs[0].shape[1], w_ref.shape[1] // me.shape[1]
    for index in range(me.shape[1]):

        @pl.when(me[0, 0] == index)
        def _(index=index):
            for slot, out in enumerate(outs):
                for core in range(2):
                    at = (index ^ (2 * slot + core)) * width
                    out[:, core * width : (core + 1) * width] = w_ref[:, at : at + width]


def run_stages(stages, blocks):
    held = [{} for _ in stages]
    for step in range(len(blocks) + 2 * len(stages)):
        for index, stage in enumerate(stages):
            at = step - 2 * index
            if 0 <= at < len(blocks):
                given = held[index - 1].pop(at) if index else ()
                held[index][at] = stage(blocks[at], *given)


def token_queries(q):
    lo, zero = low_lanes(q.shape[0]), jnp.zeros_like(q)
    return jnp.concatenate([jnp.where(lo, q, zero), jnp.where(lo, swap16(q), zero)], axis=0)


def inner_kernel(q_ref, k_ref, v_ref, x0, m0, lhs12, lhs3t, vk1, vk2, vk3, keys0, values0, scratch):
    heads, rows = q_ref.shape[0], q_ref.shape[1]
    blocks = rows // HALF
    lo = low_lanes(HALF)
    pairs, fours = group_matrix(HALF, 1), group_matrix(HALF, 2)

    shared = {}

    def start(task):
        head, block = task
        if block == 0:
            for index in range(blocks):
                at = slice(index * HALF, (index + 1) * HALF)
                put_pairs(keys0.at[head], values0.at[head], index, k_ref[head, at, :], v_ref[head, at, :])
            wide = jnp.concatenate([q_ref[head, i * HALF : (i + 1) * HALF, :] for i in range(blocks)], axis=1)
            wide2 = jnp.dot(pairs, wide, preferred_element_type=F32)
            wide3 = jnp.dot(fours, wide, preferred_element_type=F32)
            q_top = jnp.sum(q_ref[head].astype(F32), axis=0, keepdims=True)
            shared[head] = wide2, wide3, (q_top + swap(q_top)) * POOL ** (-0.5)
        if block == 4:
            sums = fold_pairs(v_ref[head], k_ref[head])
            for level, out in enumerate((vk1, vk2, vk3), 1):
                if level > 1:
                    sums = halve(scratch.at[head], sums)
                out[head] = pooled_vk(sums, 2**level)
        return ()

    def scores(task):
        head, block = task
        at, lanes = slice(block * HALF, (block + 1) * HALF), slice(block * LANES, (block + 1) * LANES)
        wide2, wide3, q_top = shared[head]
        q1, q2, q3 = (
            (sums + swap(sums)) * factor ** (-0.5)
            for sums, factor in ((q_ref[head, at, :].astype(F32), 2), (wide2[:, lanes], 4), (wide3[:, lanes], 8))
        )
        lhs12[head, at, :] = jnp.where(lo, q2, q1).astype(BF16)
        lhs3t[head, at, :] = jnp.where(lo, q_top, q3).astype(BF16)
        if block in (0, blocks - 1):
            return (None,)
        return (scores_of(token_queries(q_ref[head, at, :]), keys0[head, (block - 1) * NR : (block + 2) * NR, :]),)

    def weights(task, s0):
        if s0 is None:
            return None, None
        m = jnp.max(s0, axis=1, keepdims=True)
        return m, jnp.exp2((s0 - m) * SCALE2).astype(BF16)

    def products(task, m, p0):
        head, block = task
        if m is None:
            return
        at, window = slice((block - 1) * NR, block * NR), slice((block - 1) * NR, (block + 2) * NR)
        x0[head, at, :] = jnp.dot(p0, values0[head, window, :], preferred_element_type=F32)
        m0[head, at, :] = jnp.broadcast_to(m, (NR, LANES))

    run_stages((start, scores, weights, products), [(head, block) for head in range(heads) for block in range(blocks)])


def attend_kernel(
    head, q_ref, k_ref, v_ref, x0_in, m0_in, lhs12, lhs3t, vk1, vk2, vk3, first_in, second_in, tops, place,
    att, keys0, values0, halo_vk, scratch,
):
    own, rows = (vk1, vk2, vk3), q_ref.shape[1]
    blocks = rows // HALF
    even = lax.rem(place[0], 2) == 0
    for low in (True, False):

        def halo(index):
            at = slice(index * FAR, (index + 1) * FAR)
            sources = (second_in, first_in) if low else (first_in, second_in)
            return jnp.where(even, sources[0][head, at, :], sources[1][head, at, :])

        k, v = halo(0), halo(1)
        sums = fold_pairs(v, k)
        for level in range(1, LEVELS + 1):
            if level > 1:
                sums = halve(scratch, jnp.concatenate([beyond, sums] if low else [sums, beyond], axis=0))
            far = halo(level + 1)
            base = (2 * level - 2 + (not low)) * NR
            near_at, far_at = (base + FAR, base) if low else (base, base + FAR)
            halo_vk[near_at : near_at + HALF, :] = pooled_vk(sums, 2**level)
            halo_vk[far_at : far_at + FAR, :] = far
            beyond = far.astype(F32) * jnp.where(low_lanes(1), 2.0**level, 2.0 ** (level / 2))
        put_pairs(keys0, values0, 0 if low else 5, k, v)
        for index in range(2):
            start = index * HALF if low else rows - (2 - index) * HALF
            at = slice(start, start + HALF)
            put_pairs(keys0, values0, index + (1 if low else 3), k_ref[head, at, :], v_ref[head, at, :])

    def kept(level, half):
        mine = own[level - 1]
        count, at = mine.shape[1], (half // 2) * NR - NR
        spans = [(at, HALF), (at + 2 * NR, NR)] if half % 2 == 0 else [(at, NR), (at + 2 * NR + HALF, HALF)]
        pieces = []
        for start, size in spans:
            if 0 <= start < count:
                pieces.append(mine[head, start : start + size, :])
            else:
                start += (2 * level - 1) * NR - (count if start > 0 else 0)
                pieces.append(halo_vk[start : start + size, :])
        return jnp.concatenate(pieces, axis=0)

    def side_by_side(upper, lower):
        left = jnp.concatenate([upper, jnp.zeros((upper.shape[0], LANES), BF16)], axis=1)
        right = jnp.concatenate([jnp.zeros((lower.shape[0], LANES), BF16), lower], axis=1)
        return jnp.concatenate([left, right], axis=0)

    top = tops[head]
    positions = top.shape[0]
    lane = lax.broadcasted_iota(jnp.int32, (HALF, LANES), 1)
    distance = lane - HEAD_DIM - place[0]
    distance = jnp.where(distance < 0, distance + positions, distance)
    keep = (lane < HEAD_DIM) | ((distance >= 2) & (distance <= positions - 2))
    lo = low_lanes(HALF)

    def edge_window(block):
        return slice(0, 3 * NR) if block == 0 else slice(3 * NR, 6 * NR)

    def apart(x):
        low, zero = low_lanes(x.shape[0]), jnp.zeros_like(x)
        return jnp.concatenate([jnp.where(low, zero, x), jnp.where(low, zero, swap16(x))], axis=1)

    shared, shared_x, waiting, unfinished = {}, {}, [], []

    def scores(block):
        at = slice(block * HALF, (block + 1) * HALF)
        s12 = scores_of(apart(lhs12[head, at, :]), side_by_side(kept(1, block), kept(2, block // 2)))
        if block % 4 == 0:
            four = slice(block * HALF, (block + 4) * HALF)
            shared[block // 4] = scores_of(apart(lhs3t[head, four, :]), side_by_side(kept(3, block // 4), top))
        s3t = shared[block // 4][(block % 4) * HALF : (block % 4 + 1) * HALF]
        s0 = None
        if block in (0, blocks - 1):
            s0 = scores_of(token_queries(q_ref[head, at, :]), keys0[edge_window(block), :])
        return s0, s12, s3t

    def weights(block, s0, s12, s3t):
        masked = jnp.where(keep, s3t[:, LANES:], -jnp.inf)
        su = jnp.concatenate([s12, s3t[:, :LANES], masked], axis=1)
        mu = jnp.max(su, axis=1, keepdims=True)
        pu = jnp.exp2((su - mu) * SCALE2).astype(BF16)
        mu = jnp.concatenate([mu, mu], axis=0)
        if s0 is None:
            m0 = m0_in[head, (block - 1) * NR : block * NR, :]
            m = jnp.maximum(m0, mu)
            return None, jnp.exp2((m0 - m) * SCALE2), pu, jnp.exp2((mu - m) * SCALE2)
        m = jnp.maximum(jnp.max(s0, axis=1, keepdims=True), mu)
        return jnp.exp2((s0 - m) * SCALE2).astype(BF16), None, pu, jnp.exp2((mu - m) * SCALE2)

    def products(block, p0, share0, pu, share):
        values = ones_high(jnp.concatenate([kept(1, block), kept(2, block // 2)], axis=0))
        split = values.shape[0]
        xu = jnp.dot(pu[:, :split], values, preferred_element_type=F32)
        waiting.append(pu[:, split:])
        if block % 4 == 3:
            values = ones_high(jnp.concatenate([kept(3, block // 4), top], axis=0))
            shared_x[block // 4] = jnp.dot(jnp.concatenate(waiting, axis=0), values, preferred_element_type=F32)
            waiting.clear()
        if p0 is None:
            x = x0_in[head, (block - 1) * NR : block * NR, :] * share0
        else:
            x = jnp.dot(p0, values0[edge_window(block), :], preferred_element_type=F32)
        return x, xu, share

    def finish(block, x, xu, share):
        unfinished.append((block, x, xu, share))
        if block % 4 == 3:
            for item in unfinished:
                finish_one(*item)
            unfinished.clear()

    def finish_one(block, x, xu, share):
        xu = xu + shared_x[block // 4][(block % 4) * HALF : (block % 4 + 1) * HALF]
        x = x + jnp.concatenate([xu, xu], axis=0) * share
        x = x / swap(x)
        out = jnp.where(lo, x[:HALF], swap(x[HALF:]))
        att[0, block * HALF : (block + 1) * HALF, :] = out.astype(BF16)

    run_stages((scores, weights, products, finish), range(blocks))


def pair_weights(source, head, group):
    piece = source[head * HEAD_DIM : (head + 1) * HEAD_DIM, group * HEAD_DIM : (group + 1) * HEAD_DIM]
    zero = jnp.zeros_like(piece)
    return jnp.concatenate(
        [jnp.concatenate([piece, zero], axis=1), jnp.concatenate([zero, piece], axis=1)], axis=0
    )


def project_kernel(terms, *refs):
    count = len(terms)
    att, w, rest = refs[:count], refs[count : count + 2], refs[count + 2 :]
    earlier, outs = (rest[:2], rest[2:]) if len(rest) > 2 else (None, rest)
    heads = outs[0].shape[0]
    rows = jnp.concatenate([ref[...] for ref in att], axis=1)
    for core, out in enumerate(outs):
        for group in range(heads):
            columns = [pair_weights(w[source][...], head, core * heads + group) for source, head in terms]
            total = jnp.dot(rows, jnp.concatenate(columns, axis=0), preferred_element_type=F32)
            if earlier:
                total = total + earlier[core][group]
            out[group] = total.astype(out.dtype)


def add_kernel(mine, other, out, total, written):
    copies = []
    for head in range(total.shape[0]):
        total[head] = (mine[head] + other[head].astype(F32)).astype(BF16)
        copies.append(pltpu.make_async_copy(total.at[head], out.at[head], written.at[head]))
        copies[-1].start()
    for copy in copies:
        copy.wait()


def ring(count, step):
    return [(i, (i + step) % count) for i in range(count)]


def exchange(x, axis, bit):
    return lax.ppermute(x, axis, [(i, i ^ bit) for i in range(lax.axis_size(axis))])


def on_device(queries, keys, values, w_out):
    q, k, v = (jnp.transpose(x, (1, 0, 2)) for x in (queries, keys, values))
    heads, rows, _ = q.shape
    groups, count = lax.axis_size("head"), lax.axis_size("seq")
    params = pltpu.CompilerParams(vmem_limit_bytes=VMEM)
    vmem = pl.BlockSpec(memory_space=pltpu.VMEM)

    def shape(size, dtype=BF16):
        return jax.ShapeDtypeStruct((heads, size, LANES), dtype)

    place = lax.axis_index("seq").astype(jnp.int32).reshape(1)
    smem = pl.BlockSpec(memory_space=pltpu.SMEM)
    top, first_out, second_out = pl.pallas_call(
        prepare_kernel,
        in_specs=[pl.BlockSpec(memory_space=pltpu.HBM)] * 2 + [smem],
        out_specs=[vmem] * 3,
        out_shape=[jax.ShapeDtypeStruct((count, heads, LANES), BF16)] + [shape(HALO_ROWS)] * 2,
        scratch_shapes=[pltpu.VMEM((heads, rows, LANES), BF16)] * 2
        + [pltpu.VMEM((heads, rows, LANES), F32), pltpu.SemaphoreType.DMA((heads, 2))],
        compiler_params=pltpu.CompilerParams(vmem_limit_bytes=60 * 1024 * 1024),
        name="prepare",
    )(k, v, place)
    first_in = exchange(first_out, "seq", 1)
    second_in = lax.ppermute(second_out, "seq", [(i, (i - 1 if i % 2 == 0 else i + 1) % count) for i in range(count)])
    tops = lax.all_to_all(top, "seq", split_axis=0, concat_axis=0, tiled=True).transpose(1, 0, 2)
    top, w_out = lax.optimization_barrier((top, w_out))
    width = w_out.shape[1] // groups
    me = jnp.full((1, groups), lax.axis_index("head"), jnp.int32)
    w_own, w_far = pl.pallas_call(
        cut_kernel,
        in_specs=[vmem, pl.BlockSpec(memory_space=pltpu.SMEM)],
        out_specs=[vmem] * 2,
        out_shape=[jax.ShapeDtypeStruct((w_out.shape[0], 2 * width), BF16)] * 2,
        compiler_params=params,
        name="cut",
    )(w_out, me)
    w_far = exchange(w_far, "head", 2)

    tops, first_in, q = lax.optimization_barrier((tops, first_in, q))
    pooled = [rows >> level for level in range(LEVELS)]
    inner = pl.pallas_call(
        inner_kernel,
        in_specs=[vmem] * 3,
        out_specs=[vmem] * 7,
        out_shape=[shape(2 * rows - 2 * NR, F32)] * 2 + [shape(rows)] * 2 + [shape(size) for size in pooled],
        scratch_shapes=[pltpu.VMEM((heads, 2 * rows, LANES), BF16)] * 2 + [pltpu.VMEM((heads, rows, LANES), F32)],
        compiler_params=params,
        cost_estimate=pl.CostEstimate(flops=4_000_000_000, bytes_accessed=8_000_000, transcendentals=1_000_000),
        name="inner",
    )(q, k, v)
    parts = {}
    for head in range(heads):
        att = pl.pallas_call(
            functools.partial(attend_kernel, head),
            in_specs=[vmem] * 13 + [smem],
            out_specs=vmem,
            out_shape=jax.ShapeDtypeStruct((1, rows, LANES), BF16),
            scratch_shapes=[pltpu.VMEM((6 * NR, LANES), BF16)] * 3 + [pltpu.VMEM((NR, LANES), F32)],
            compiler_params=params,
            name=f"attend{head}",
        )(q, k, v, *inner, first_in, second_in, tops, place)[0]
        parts[0, head], parts[1, head] = att, exchange(att, "head", 2)
    late = [(1, LAST)]
    early = [term for term in parts if term not in late]
    shares = []
    for terms, types in ((early, (F32, F32)), (late, (F32, BF16))):
        shares = pl.pallas_call(
            functools.partial(project_kernel, terms),
            in_specs=[vmem] * (len(terms) + 2 + len(shares)),
            out_specs=[vmem] * 2,
            out_shape=[shape(rows, dtype) for dtype in types],
            compiler_params=params,
            name="project",
        )(*[parts[term] for term in terms], w_own, w_far, *shares)
    out = pl.pallas_call(
        add_kernel,
        in_specs=[vmem] * 2,
        out_specs=pl.BlockSpec(memory_space=pltpu.HBM),
        scratch_shapes=[pltpu.VMEM((heads, rows, LANES), BF16), pltpu.SemaphoreType.DMA((heads,))],
        out_shape=shape(rows),
        compiler_params=params,
        name="add",
    )(shares[0], exchange(shares[1], "head", 1))
    return jnp.transpose(out, (1, 0, 2))


def solution(mesh):
    return jax.shard_map(
        on_device,
        mesh=mesh,
        in_specs=(
            P("seq", "head", None),
            P("seq", "head", None),
            P("seq", "head", None),
            P("head", None),
        ),
        out_specs=P("seq", "head", None),
        check_vma=False,
    )
```

```python
import functools
import math

import jax
import jax.numpy as jnp
from jax import lax
from jax.experimental import pallas as pl
from jax.experimental.pallas import tpu as pltpu
from jax.sharding import PartitionSpec as P

HEAD_DIM = 64
NR = 128
HALF = NR // 2
LANES = 2 * HEAD_DIM
LEVELS = 3
POOL = 1024
BF16 = jnp.bfloat16
F32 = jnp.float32
SCALE2 = HEAD_DIM ** (-0.5) * math.log2(math.e)
FAR = HALF
VMEM = 16 * 1024 * 1024
LAST = 2
HALO_ROWS = 2 * HALF + LEVELS * FAR


def low_lanes(rows):
    return lax.broadcasted_iota(jnp.int32, (rows, LANES), 1) < HEAD_DIM


def swap(x):
    return pltpu.roll(x, HEAD_DIM, 1)


def swap16(x):
    return pltpu.roll(x, HEAD_DIM, 1)


def fold_pairs(lo, hi):
    lo, hi = lo.astype(F32), hi.astype(F32)
    return jnp.where(low_lanes(lo.shape[0]), lo + swap(lo), hi + swap(hi))


def halve(scratch, x):
    rows = x.shape[0]
    scratch[pl.ds(0, rows), :] = x
    return scratch[pl.ds(0, rows // 2, 2), :] + scratch[pl.ds(1, rows // 2, 2), :]


def pooled_vk(sums, factor):
    scale = jnp.where(low_lanes(1), 1.0 / factor, factor ** (-0.5))
    return (sums * scale).astype(BF16)


def ones_high(v):
    return jnp.where(low_lanes(v.shape[0]), v, jnp.ones_like(v))


def put_pairs(keys, values, block, k, v):
    at = block * NR
    keys[at : at + HALF, :] = k
    keys[at + HALF : at + NR, :] = swap16(k)
    values[at : at + HALF, :] = ones_high(v)
    values[at + HALF : at + NR, :] = ones_high(swap16(v))


def scores_of(lhs, keys):
    return lax.dot_general(lhs, keys, (((1,), (1,)), ((), ())), preferred_element_type=F32)


def group_matrix(rows, shift):
    group = [lax.broadcasted_iota(jnp.int32, (rows, rows), axis) >> shift for axis in range(2)]
    return jnp.where(group[0] == group[1], 1.0, 0.0).astype(BF16)


def prepare_kernel(k_hbm, v_hbm, place, top, first_out, second_out, k, v, scratch, read):
    heads, rows = k.shape[0], k.shape[1]
    even = lax.rem(place[0], 2) == 0
    loads = [
        [
            pltpu.make_async_copy(source.at[head], into.at[head], read.at[head, index])
            for index, (source, into) in enumerate(((k_hbm, k), (v_hbm, v)))
        ]
        for head in range(heads)
    ]
    for pair in loads:
        for copy in pair:
            copy.start()
    coarse = []
    for head in range(heads):
        for copy in loads[head]:
            copy.wait()
        lows, highs = [], []
        for source in (k, v):
            lows.append(source[head, 0:HALF, :])
            highs.append(source[head, rows - HALF : rows, :])
        sums = fold_pairs(v[head], k[head])
        for level in range(1, LEVELS + 1):
            if level > 1:
                sums = halve(scratch.at[head], sums)
            vk = pooled_vk(sums, 2**level)
            lows.append(vk[HALF : HALF + FAR])
            highs.append(vk[vk.shape[0] - HALF - FAR : vk.shape[0] - HALF])
        for index, (low, high) in enumerate(zip(lows, highs)):
            at = slice(index * FAR, (index + 1) * FAR)
            first_out[head, at, :] = jnp.where(even, high, low)
            second_out[head, at, :] = jnp.where(even, low, high)
        coarse.append(jnp.sum(sums, axis=0, keepdims=True))
    rows = pooled_vk(jnp.concatenate(coarse, axis=0), POOL)
    for position in range(top.shape[0]):
        top[position] = rows


def cut_kernel(w_ref, me, *outs):
    half, width = outs[0].shape[1], w_ref.shape[1] // me.shape[1]
    for index in range(me.shape[1]):

        @pl.when(me[0, 0] == index)
        def _(index=index):
            for slot, out in enumerate(outs):
                for core in range(2):
                    at = (index ^ (2 * slot + core)) * width
                    out[:, core * width : (core + 1) * width] = w_ref[:, at : at + width]


def run_stages(stages, blocks):
    held = [{} for _ in stages]
    for step in range(len(blocks) + 3 * len(stages)):
        for index, stage in enumerate(stages):
            at = step - 3 * index
            if 0 <= at < len(blocks):
                given = held[index - 1].pop(at) if index else ()
                held[index][at] = stage(blocks[at], *given)


def token_queries(q):
    lo, zero = low_lanes(q.shape[0]), jnp.zeros_like(q)
    return jnp.concatenate([jnp.where(lo, q, zero), jnp.where(lo, swap16(q), zero)], axis=0)


def inner_kernel(q_ref, k_ref, v_ref, x0, m0, lhs12, lhs3t, vk1, vk2, vk3, keys0, values0, scratch):
    heads, rows = q_ref.shape[0], q_ref.shape[1]
    blocks = rows // HALF
    lo = low_lanes(HALF)
    pairs, fours = group_matrix(HALF, 1), group_matrix(HALF, 2)

    shared = {}

    def start(task):
        head, block = task
        if block == 0:
            for index in range(blocks):
                at = slice(index * HALF, (index + 1) * HALF)
                put_pairs(keys0.at[head], values0.at[head], index, k_ref[head, at, :], v_ref[head, at, :])
            wide = jnp.concatenate([q_ref[head, i * HALF : (i + 1) * HALF, :] for i in range(blocks)], axis=1)
            wide2 = jnp.dot(pairs, wide, preferred_element_type=F32)
            wide3 = jnp.dot(fours, wide, preferred_element_type=F32)
            q_top = jnp.sum(q_ref[head].astype(F32), axis=0, keepdims=True)
            shared[head] = wide2, wide3, (q_top + swap(q_top)) * POOL ** (-0.5)
        if block == 4:
            sums = fold_pairs(v_ref[head], k_ref[head])
            for level, out in enumerate((vk1, vk2, vk3), 1):
                if level > 1:
                    sums = halve(scratch.at[head], sums)
                out[head] = pooled_vk(sums, 2**level)
        return ()

    def scores(task):
        head, block = task
        at, lanes = slice(block * HALF, (block + 1) * HALF), slice(block * LANES, (block + 1) * LANES)
        wide2, wide3, q_top = shared[head]
        q1, q2, q3 = (
            (sums + swap(sums)) * factor ** (-0.5)
            for sums, factor in ((q_ref[head, at, :].astype(F32), 2), (wide2[:, lanes], 4), (wide3[:, lanes], 8))
        )
        lhs12[head, at, :] = jnp.where(lo, q2, q1).astype(BF16)
        lhs3t[head, at, :] = jnp.where(lo, q_top, q3).astype(BF16)
        if block in (0, blocks - 1):
            return (None,)
        return (scores_of(token_queries(q_ref[head, at, :]), keys0[head, (block - 1) * NR : (block + 2) * NR, :]),)

    def weights(task, s0):
        if s0 is None:
            return None, None
        m = jnp.max(s0, axis=1, keepdims=True)
        return m, jnp.exp2((s0 - m) * SCALE2).astype(BF16)

    def products(task, m, p0):
        head, block = task
        if m is None:
            return
        at, window = slice((block - 1) * NR, block * NR), slice((block - 1) * NR, (block + 2) * NR)
        x0[head, at, :] = jnp.dot(p0, values0[head, window, :], preferred_element_type=F32)
        m0[head, at, :] = jnp.broadcast_to(m, (NR, LANES))

    run_stages((start, scores, weights, products), [(head, block) for head in range(heads) for block in range(blocks)])


def attend_kernel(
    head, q_ref, k_ref, v_ref, x0_in, m0_in, lhs12, lhs3t, vk1, vk2, vk3, first_in, second_in, tops, place,
    att, keys0, values0, halo_vk, scratch,
):
    own, rows = (vk1, vk2, vk3), q_ref.shape[1]
    blocks = rows // HALF
    even = lax.rem(place[0], 2) == 0
    for low in (True, False):

        def halo(index):
            at = slice(index * FAR, (index + 1) * FAR)
            sources = (second_in, first_in) if low else (first_in, second_in)
            return jnp.where(even, sources[0][head, at, :], sources[1][head, at, :])

        k, v = halo(0), halo(1)
        sums = fold_pairs(v, k)
        for level in range(1, LEVELS + 1):
            if level > 1:
                sums = halve(scratch, jnp.concatenate([beyond, sums] if low else [sums, beyond], axis=0))
            far = halo(level + 1)
            base = (2 * level - 2 + (not low)) * NR
            near_at, far_at = (base + FAR, base) if low else (base, base + FAR)
            halo_vk[near_at : near_at + HALF, :] = pooled_vk(sums, 2**level)
            halo_vk[far_at : far_at + FAR, :] = far
            beyond = far.astype(F32) * jnp.where(low_lanes(1), 2.0**level, 2.0 ** (level / 2))
        put_pairs(keys0, values0, 0 if low else 5, k, v)
        for index in range(2):
            start = index * HALF if low else rows - (2 - index) * HALF
            at = slice(start, start + HALF)
            put_pairs(keys0, values0, index + (1 if low else 3), k_ref[head, at, :], v_ref[head, at, :])

    def kept(level, half):
        mine = own[level - 1]
        count, at = mine.shape[1], (half // 2) * NR - NR
        spans = [(at, HALF), (at + 2 * NR, NR)] if half % 2 == 0 else [(at, NR), (at + 2 * NR + HALF, HALF)]
        pieces = []
        for start, size in spans:
            if 0 <= start < count:
                pieces.append(mine[head, start : start + size, :])
            else:
                start += (2 * level - 1) * NR - (count if start > 0 else 0)
                pieces.append(halo_vk[start : start + size, :])
        return jnp.concatenate(pieces, axis=0)

    def side_by_side(upper, lower):
        left = jnp.concatenate([upper, jnp.zeros((upper.shape[0], LANES), BF16)], axis=1)
        right = jnp.concatenate([jnp.zeros((lower.shape[0], LANES), BF16), lower], axis=1)
        return jnp.concatenate([left, right], axis=0)

    top = tops[head]
    positions = top.shape[0]
    lane = lax.broadcasted_iota(jnp.int32, (HALF, LANES), 1)
    distance = lane - HEAD_DIM - place[0]
    distance = jnp.where(distance < 0, distance + positions, distance)
    keep = (lane < HEAD_DIM) | ((distance >= 2) & (distance <= positions - 2))
    lo = low_lanes(HALF)

    def edge_window(block):
        return slice(0, 3 * NR) if block == 0 else slice(3 * NR, 6 * NR)

    def apart(x):
        low, zero = low_lanes(x.shape[0]), jnp.zeros_like(x)
        return jnp.concatenate([jnp.where(low, zero, x), jnp.where(low, zero, swap16(x))], axis=1)

    shared, shared_x, waiting, unfinished = {}, {}, [], []

    def scores(block):
        at = slice(block * HALF, (block + 1) * HALF)
        s12 = scores_of(apart(lhs12[head, at, :]), side_by_side(kept(1, block), kept(2, block // 2)))
        if block % 4 == 0:
            four = slice(block * HALF, (block + 4) * HALF)
            shared[block // 4] = scores_of(apart(lhs3t[head, four, :]), side_by_side(kept(3, block // 4), top))
        s3t = shared[block // 4][(block % 4) * HALF : (block % 4 + 1) * HALF]
        s0 = None
        if block in (0, blocks - 1):
            s0 = scores_of(token_queries(q_ref[head, at, :]), keys0[edge_window(block), :])
        return s0, s12, s3t

    def weights(block, s0, s12, s3t):
        masked = jnp.where(keep, s3t[:, LANES:], -jnp.inf)
        su = jnp.concatenate([s12, s3t[:, :LANES], masked], axis=1)
        mu = jnp.max(su, axis=1, keepdims=True)
        pu = jnp.exp2((su - mu) * SCALE2).astype(BF16)
        mu = jnp.concatenate([mu, mu], axis=0)
        if s0 is None:
            m0 = m0_in[head, (block - 1) * NR : block * NR, :]
            m = jnp.maximum(m0, mu)
            return None, jnp.exp2((m0 - m) * SCALE2), pu, jnp.exp2((mu - m) * SCALE2)
        m = jnp.maximum(jnp.max(s0, axis=1, keepdims=True), mu)
        return jnp.exp2((s0 - m) * SCALE2).astype(BF16), None, pu, jnp.exp2((mu - m) * SCALE2)

    def products(block, p0, share0, pu, share):
        values = ones_high(jnp.concatenate([kept(1, block), kept(2, block // 2)], axis=0))
        split = values.shape[0]
        xu = jnp.dot(pu[:, :split], values, preferred_element_type=F32)
        waiting.append(pu[:, split:])
        if block % 4 == 3:
            values = ones_high(jnp.concatenate([kept(3, block // 4), top], axis=0))
            shared_x[block // 4] = jnp.dot(jnp.concatenate(waiting, axis=0), values, preferred_element_type=F32)
            waiting.clear()
        if p0 is None:
            x = x0_in[head, (block - 1) * NR : block * NR, :] * share0
        else:
            x = jnp.dot(p0, values0[edge_window(block), :], preferred_element_type=F32)
        return x, xu, share

    def finish(block, x, xu, share):
        unfinished.append((block, x, xu, share))
        if block % 4 == 3:
            for item in unfinished:
                finish_one(*item)
            unfinished.clear()

    def finish_one(block, x, xu, share):
        xu = xu + shared_x[block // 4][(block % 4) * HALF : (block % 4 + 1) * HALF]
        x = x + jnp.concatenate([xu, xu], axis=0) * share
        x = x / swap(x)
        out = jnp.where(lo, x[:HALF], swap(x[HALF:]))
        att[0, block * HALF : (block + 1) * HALF, :] = out.astype(BF16)

    run_stages((scores, weights, products, finish), range(blocks))


def pair_weights(source, head, group):
    piece = source[head * HEAD_DIM : (head + 1) * HEAD_DIM, group * HEAD_DIM : (group + 1) * HEAD_DIM]
    zero = jnp.zeros_like(piece)
    return jnp.concatenate(
        [jnp.concatenate([piece, zero], axis=1), jnp.concatenate([zero, piece], axis=1)], axis=0
    )


def project_kernel(terms, *refs):
    count = len(terms)
    att, w, rest = refs[:count], refs[count : count + 2], refs[count + 2 :]
    earlier, outs = (rest[:2], rest[2:]) if len(rest) > 2 else (None, rest)
    heads = outs[0].shape[0]
    rows = jnp.concatenate([ref[...] for ref in att], axis=1)
    for core, out in enumerate(outs):
        for group in range(heads):
            columns = [pair_weights(w[source][...], head, core * heads + group) for source, head in terms]
            total = jnp.dot(rows, jnp.concatenate(columns, axis=0), preferred_element_type=F32)
            if earlier:
                total = total + earlier[core][group]
            out[group] = total.astype(out.dtype)


def add_kernel(mine, other, out, total, written):
    copies = []
    for head in range(total.shape[0]):
        total[head] = (mine[head] + other[head].astype(F32)).astype(BF16)
        copies.append(pltpu.make_async_copy(total.at[head], out.at[head], written.at[head]))
        copies[-1].start()
    for copy in copies:
        copy.wait()


def ring(count, step):
    return [(i, (i + step) % count) for i in range(count)]


def exchange(x, axis, bit):
    return lax.ppermute(x, axis, [(i, i ^ bit) for i in range(lax.axis_size(axis))])


def on_device(queries, keys, values, w_out):
    q, k, v = (jnp.transpose(x, (1, 0, 2)) for x in (queries, keys, values))
    heads, rows, _ = q.shape
    groups, count = lax.axis_size("head"), lax.axis_size("seq")
    params = pltpu.CompilerParams(vmem_limit_bytes=VMEM)
    vmem = pl.BlockSpec(memory_space=pltpu.VMEM)

    def shape(size, dtype=BF16):
        return jax.ShapeDtypeStruct((heads, size, LANES), dtype)

    place = lax.axis_index("seq").astype(jnp.int32).reshape(1)
    smem = pl.BlockSpec(memory_space=pltpu.SMEM)
    top, first_out, second_out = pl.pallas_call(
        prepare_kernel,
        in_specs=[pl.BlockSpec(memory_space=pltpu.HBM)] * 2 + [smem],
        out_specs=[vmem] * 3,
        out_shape=[jax.ShapeDtypeStruct((count, heads, LANES), BF16)] + [shape(HALO_ROWS)] * 2,
        scratch_shapes=[pltpu.VMEM((heads, rows, LANES), BF16)] * 2
        + [pltpu.VMEM((heads, rows, LANES), F32), pltpu.SemaphoreType.DMA((heads, 2))],
        compiler_params=pltpu.CompilerParams(vmem_limit_bytes=60 * 1024 * 1024),
        name="prepare",
    )(k, v, place)
    first_in = exchange(first_out, "seq", 1)
    second_in = lax.ppermute(second_out, "seq", [(i, (i - 1 if i % 2 == 0 else i + 1) % count) for i in range(count)])
    tops = lax.all_to_all(top, "seq", split_axis=0, concat_axis=0, tiled=True).transpose(1, 0, 2)
    top, w_out = lax.optimization_barrier((top, w_out))
    width = w_out.shape[1] // groups
    me = jnp.full((1, groups), lax.axis_index("head"), jnp.int32)
    w_own, w_far = pl.pallas_call(
        cut_kernel,
        in_specs=[vmem, pl.BlockSpec(memory_space=pltpu.SMEM)],
        out_specs=[vmem] * 2,
        out_shape=[jax.ShapeDtypeStruct((w_out.shape[0], 2 * width), BF16)] * 2,
        compiler_params=params,
        name="cut",
    )(w_out, me)
    w_far = exchange(w_far, "head", 2)

    tops, first_in, q = lax.optimization_barrier((tops, first_in, q))
    pooled = [rows >> level for level in range(LEVELS)]
    inner = pl.pallas_call(
        inner_kernel,
        in_specs=[vmem] * 3,
        out_specs=[vmem] * 7,
        out_shape=[shape(2 * rows - 2 * NR, F32)] * 2 + [shape(rows)] * 2 + [shape(size) for size in pooled],
        scratch_shapes=[pltpu.VMEM((heads, 2 * rows, LANES), BF16)] * 2 + [pltpu.VMEM((heads, rows, LANES), F32)],
        compiler_params=params,
        cost_estimate=pl.CostEstimate(flops=4_000_000_000, bytes_accessed=8_000_000, transcendentals=1_000_000),
        name="inner",
    )(q, k, v)
    parts = {}
    for head in range(heads):
        att = pl.pallas_call(
            functools.partial(attend_kernel, head),
            in_specs=[vmem] * 13 + [smem],
            out_specs=vmem,
            out_shape=jax.ShapeDtypeStruct((1, rows, LANES), BF16),
            scratch_shapes=[pltpu.VMEM((6 * NR, LANES), BF16)] * 3 + [pltpu.VMEM((NR, LANES), F32)],
            compiler_params=params,
            name=f"attend{head}",
        )(q, k, v, *inner, first_in, second_in, tops, place)[0]
        parts[0, head], parts[1, head] = att, exchange(att, "head", 2)
    late = [(1, LAST)]
    early = [term for term in parts if term not in late]
    shares = []
    for terms, types in ((early, (F32, F32)), (late, (F32, BF16))):
        shares = pl.pallas_call(
            functools.partial(project_kernel, terms),
            in_specs=[vmem] * (len(terms) + 2 + len(shares)),
            out_specs=[vmem] * 2,
            out_shape=[shape(rows, dtype) for dtype in types],
            compiler_params=params,
            name="project",
        )(*[parts[term] for term in terms], w_own, w_far, *shares)
    out = pl.pallas_call(
        add_kernel,
        in_specs=[vmem] * 2,
        out_specs=pl.BlockSpec(memory_space=pltpu.HBM),
        scratch_shapes=[pltpu.VMEM((heads, rows, LANES), BF16), pltpu.SemaphoreType.DMA((heads,))],
        out_shape=shape(rows),
        compiler_params=params,
        name="add",
    )(shares[0], exchange(shares[1], "head", 1))
    return jnp.transpose(out, (1, 0, 2))


def solution(mesh):
    return jax.shard_map(
        on_device,
        mesh=mesh,
        in_specs=(
            P("seq", "head", None),
            P("seq", "head", None),
            P("seq", "head", None),
            P("head", None),
        ),
        out_specs=P("seq", "head", None),
        check_vma=False,
    )
```
